128 devices in a mesh: seq: 8 (over z, core), exp: 16 (over x, y).
Axes of the slice: x: 4, y: 4, z: 4, core: 2. Of those that a mesh axis runs over, the one named last changes fastest.
Arguments:
- queries: bfloat16 [8192, 4096], P('seq', 'exp'), may hold values from -6 to 6
- keys: bfloat16 [8192, 4096], P('seq', 'exp'), may hold values from -6 to 6
- values: bfloat16 [8192, 4096], P('seq', 'exp'), may hold values from -6 to 6
- gates: int32 [8, 3], replicated, may hold values from 0 to 7, as said below
- o_proj: bfloat16 [4096, 3584], P('exp'), may hold values from -0.5 to 0.5
- residual: bfloat16 [8192, 3584], P(('seq', 'exp')), may hold values from -40 to 40
- norm_gain: float32 [3584], replicated, may hold values from 0.25 to 1.75
- routes: int32 [8192, 8], P(('seq', 'exp')), may hold values from 0 to 127, all different within a row; in each aligned block of 64 rows (0 to 63, 64 to 127, ...) at most 8 rows name the same one
- route_weights: float32 [8192, 8], P(('seq', 'exp')), may hold values from 0.05 to 0.5
- w_gate: bfloat16 [128, 3584, 1024], P(('seq', 'exp')), may hold values from -0.09375 to 0.09375
- w_up: bfloat16 [128, 3584, 1024], P(('seq', 'exp')), may hold values from -0.09375 to 0.09375
- w_down: bfloat16 [128, 1024, 3584], P(('seq', 'exp')), may hold values from -0.1875 to 0.1875
Outputs:
- attn_proj: bfloat16 [8192, 3584], P(('seq', 'exp'))
- moe_out: bfloat16 [8192, 3584], P(('seq', 'exp'))
The draws below stay inside these ranges and needn't reach their ends.
Inputs may be any that keep to these rules, and one draw needn't show every extreme that they name: `gates`: entry 0 of row b is b; every other entry is either a block below b, distinct within the row, or b itself marking an unused entry; row b names min(b, 2) blocks below b. `routes`: the 8 experts of a token are distinct; the rows of one device name each expert at most 8 times, a bound that some block reaches.
All inputs are finite; a program needn't handle non-finite values.
Results may differ from the reference program's by a relative error of at most 0.035.
Values may be sent and summed in bfloat16 or wider, within the bound.
No kernel may reach another device: no remote copies, remote signals or barrier semaphores. Data moves between devices by JAX's collectives and lax.ppermute only.
A program may use at most 128 MiB of HBM per device.

```python
import math
import jax
import jax.numpy as jnp
import numpy as np
from jax import lax

D = 3584
FF_E = 1024
HEADS = 32
HD = 128
BLOCK = 1024
TOPK = 3
ROUTE_K = 8
NBLK = 8
TOKENS = 8192
TOK_MOE = 64
EXPERTS = 128
CAP = 8
N_SEQ = 8
N_EXP = 16


def draw_queries(key, part):
    key = jax.random.fold_in(key, 1)
    full_shape = (TOKENS, HEADS * HD)
    drawn = jnp.clip(2.0 * jax.random.normal(key, full_shape, jnp.float32), -6.0, 6.0)
    return drawn.astype(jnp.bfloat16)


def draw_keys(key, part):
    key = jax.random.fold_in(key, 2)
    full_shape = (TOKENS, HEADS * HD)
    drawn = jnp.clip(jax.random.normal(key, full_shape, jnp.float32), -6.0, 6.0)
    return drawn.astype(jnp.bfloat16)


def draw_residual(key, part):
    key = jax.random.fold_in(key, 3)
    noise_key, row_key, col_key = jax.random.split(key, 3)
    row_scale = jnp.exp(jax.random.uniform(row_key, (TOKENS, 1), jnp.float32, -1.15, 1.15))
    col_scale = jnp.exp(jax.random.uniform(col_key, (1, D), jnp.float32, -1.15, 1.15))
    drawn = jax.random.normal(noise_key, (TOKENS, D), jnp.float32)
    return jnp.clip(drawn * row_scale * col_scale, -40.0, 40.0).astype(jnp.bfloat16)


def draw_gates(key, part):
    key = jax.random.fold_in(key, 4)
    block_ids = jnp.arange(NBLK, dtype=jnp.int32)
    random_part = jax.random.randint(key, (NBLK, NBLK), 0, 4096, dtype=jnp.int32)
    scores = (random_part + (NBLK - block_ids)[None, :] * 64) * NBLK + block_ids[None, :]
    earlier = block_ids[None, :] < block_ids[:, None]
    scores = jnp.where(earlier, scores, -1 - block_ids[None, :])
    top_scores, top_ids = lax.top_k(scores, TOPK - 1)
    chosen = jnp.where(top_scores >= 0, top_ids.astype(jnp.int32), block_ids[:, None])
    return jnp.concatenate([block_ids[:, None], chosen], axis=1).astype(jnp.int32)


def levels(rng, extent, cuts, least, high):
    def one(dim, blocks):
        heights = jax.random.uniform(jax.random.fold_in(jax.random.fold_in(rng, 6), dim), (blocks,), jnp.float32, least / len(cuts), high / len(cuts))
        return jnp.repeat(jnp.exp(heights), extent[dim] // blocks).reshape((-1,) + (1,) * (len(extent) - dim - 1))

    level = one(*cuts[0])
    for cut in cuts[1:]:
        level = level * one(*cut)
    return level


def assign_block(own_key, own, number, rows, number_of, top, limit, lean):
    order = jax.random.permutation(own_key, number_of)
    crowded, ordinary = shares(number_of, rows * top, limit, lean, True), shares(number_of, rows * top, limit, lean, False)
    places = jnp.arange(number_of)

    def named(tallies, rotation):
        used = int((tallies > 0).sum())
        fixed = max(1, used // 4)
        moved = fixed + (places - fixed + rotation * (used - fixed)) % max(1, number_of - fixed)
        return jnp.zeros((number_of,), jnp.int32).at[order[jnp.where(places < fixed, places, moved)]].set(jnp.asarray(tallies, jnp.int32))

    tallies = jnp.where(number % 4 == 0, named(crowded, number // 4), named(ordinary, number - number // 4 - 1))
    mixed = jax.random.permutation(jax.random.fold_in(own, 3), number_of)
    giver, sink = mixed[0:number_of // 2 * 2:2], mixed[1:number_of // 2 * 2:2]
    room = jnp.minimum(tallies[giver] - 1, limit - tallies[sink]) // 2
    room = jnp.where((giver == order[0]) | (sink == order[0]) | (tallies[sink] == 0), 0, jnp.maximum(room, 0))
    moved = jax.random.randint(jax.random.fold_in(own, 4), (number_of // 2,), 0, 1 << 20) % (room + 1)
    tallies = tallies.at[giver].add(-moved).at[sink].add(moved)
    items = jnp.searchsorted(jnp.cumsum(tallies), jnp.arange(rows * top), side="right").astype(jnp.int32)
    listing = items.reshape(top, rows).T
    listing = listing[jax.random.permutation(jax.random.fold_in(own, 1), rows)]
    rotation = jax.random.randint(jax.random.fold_in(own, 2), (rows, 1), 0, top)
    return jnp.take_along_axis(listing, (jnp.arange(top)[None, :] + rotation) % top, axis=1)


def shares(number_of, total, most, lean, full):
    loads = [(1 << 20) // math.isqrt(rank ** lean) + 1 for rank in range(1, number_of + 1)]
    largest = most if full else min(most, max(-(-total // number_of), total * loads[0] // sum(loads)))
    least = 1 if total - largest >= number_of - 1 else 0
    holding, rest = [largest] + [least] * (number_of - 1), total - largest - least * (number_of - 1)
    while rest > 0:
        movable = [i for i in range(1, number_of) if holding[i] < largest] or [i for i in range(1, number_of) if holding[i] < most]
        whole, budget = sum([loads[i] for i in movable]), rest
        for i in movable:
            extra = min(most - holding[i], max(1, budget * loads[i] // whole), rest)
            holding[i] = holding[i] + extra
            rest = rest - extra
    return np.array(holding)


def centred(own_key, dims, width, most, cuts=(), kind=jnp.bfloat16):
    array = width * jax.random.normal(own_key, dims, jnp.float32)
    if cuts:
        array = array * levels(own_key, dims, cuts, -0.22, 0.18)
    return jnp.clip(array, -most, most).astype(kind)


def setup_inputs(seed: int = 0) -> dict:
    seeds = jax.random.split(jax.random.key(seed), 13)
    queries = draw_queries(jax.random.fold_in(seeds[12], 71), 0)
    keys = draw_keys(jax.random.fold_in(seeds[12], 71), 0)
    values = centred(seeds[2], (TOKENS, HEADS * HD), 1.0, 6.0, ((0, 8), (1, 16)))
    gates = draw_gates(jax.random.fold_in(seeds[12], 71), 0)
    o_proj = centred(seeds[4], (HEADS * HD, D), (HEADS * HD // 36) ** -0.5, 0.5, ((0, 16),))
    residual = draw_residual(jax.random.fold_in(seeds[12], 71), 0)
    norm_gain = jnp.clip(1.0 + 0.15 * jax.random.normal(seeds[6], (D,), jnp.float32), 0.25, 1.75)
    routes_keys = jax.random.split(jax.random.fold_in(seeds[7], 1), TOKENS // TOK_MOE)
    routes_turns = jax.random.permutation(jax.random.fold_in(seeds[7], 3), TOKENS // TOK_MOE)
    routes = jax.vmap(lambda own, number: assign_block(jax.random.fold_in(seeds[7], 2), own, number, TOK_MOE, EXPERTS, ROUTE_K, CAP, 2))(routes_keys, routes_turns).reshape((TOKENS, ROUTE_K))
    route_weights = jnp.clip(jnp.exp(math.log(0.5) - 2.3025851 * jax.random.uniform(seeds[8], (TOKENS, ROUTE_K), jnp.float32) ** levels(seeds[8], (TOKENS, ROUTE_K), ((0, 128),), -0.2, 0.2)), 0.05, 0.5)
    w_gate = centred(seeds[9], (EXPERTS, D, FF_E), D ** -0.5, 0.09375, ((0, 128),))
    w_up = centred(seeds[10], (EXPERTS, D, FF_E), D ** -0.5, 0.09375, ((0, 128),))
    w_down = centred(seeds[11], (EXPERTS, FF_E, D), FF_E ** -0.5, 0.1875, ((0, 128),))
    return dict(queries=queries, keys=keys, values=values, gates=gates, o_proj=o_proj, residual=residual, norm_gain=norm_gain, routes=routes, route_weights=route_weights, w_gate=w_gate, w_up=w_up, w_down=w_down)


NEG_FILL = -1e+30

def rounded(values_f32):
    return lax.optimization_barrier(values_f32.astype(jnp.bfloat16)).astype(jnp.float32)

def attend_block(queries4, keys4, values4, gates, block_id):
    chosen = gates[block_id]
    query_blk = queries4[block_id]
    key_sel = keys4[chosen]
    value_sel = values4[chosen]
    slot_ids = jnp.arange(TOPK)
    counted = jnp.logical_or(slot_ids == 0, chosen != block_id)
    query_pos = lax.broadcasted_iota(jnp.int32, (BLOCK, BLOCK), 0)
    key_pos = lax.broadcasted_iota(jnp.int32, (BLOCK, BLOCK), 1)
    allowed = jnp.logical_or((slot_ids > 0)[:, None, None], (key_pos <= query_pos)[None])
    inv_root = 1.0 / math.sqrt(HD)

    def one_head(head_id):
        query_head = jnp.take(query_blk, head_id, axis=1).astype(jnp.float32)
        key_head = jnp.take(key_sel, head_id, axis=2).astype(jnp.float32)
        value_head = jnp.take(value_sel, head_id, axis=2).astype(jnp.float32)
        scores = jnp.einsum('qd,jkd->jqk', query_head, key_head) * inv_root
        masked = jnp.where(allowed, scores, NEG_FILL)
        row_max = lax.optimization_barrier(jnp.max(masked, axis=-1))
        weights = jnp.where(allowed, jnp.exp(masked - row_max[..., None]), 0.0)
        amount = lax.optimization_barrier(jnp.sum(weights, axis=-1))
        mixed_rows = jnp.einsum('jqk,jkd->jqd', rounded(weights), value_head)
        block_part = rounded(mixed_rows / amount[..., None])
        overall = lax.optimization_barrier(jnp.max(jnp.where(counted[:, None], row_max, NEG_FILL), axis=0))
        factor = jnp.where(counted[:, None], jnp.exp(row_max - overall[None]) * amount, 0.0)
        combined = lax.optimization_barrier(jnp.sum(factor[..., None] * block_part, axis=0)) / lax.optimization_barrier(jnp.sum(factor, axis=0))[:, None]
        return combined.astype(jnp.bfloat16)
    heads_out = lax.map(one_head, jnp.arange(HEADS))
    return jnp.transpose(heads_out, (1, 0, 2)).reshape(BLOCK, HEADS * HD)

def reference(queries, keys, values, gates, o_proj, residual, norm_gain, routes, route_weights, w_gate, w_up, w_down):
    shape_four = (NBLK, BLOCK, HEADS, HD)
    queries4 = queries.reshape(shape_four)
    keys4 = keys.reshape(shape_four)
    values4 = values.reshape(shape_four)
    attn = lax.map(lambda block_id: attend_block(queries4, keys4, values4, gates, block_id), jnp.arange(NBLK))
    attn = attn.reshape(TOKENS, HEADS * HD)
    group_width = HEADS * HD // N_EXP
    summed = jnp.zeros((TOKENS, D), jnp.float32)
    for group_id in range(N_EXP):
        low_col = group_id * group_width
        high_col = low_col + group_width
        summed = summed + rounded(jnp.dot(attn[:, low_col:high_col], o_proj[low_col:high_col], preferred_element_type=jnp.float32))
    attn_proj = summed.astype(jnp.bfloat16)
    residual_sum = residual.astype(jnp.float32) + attn_proj.astype(jnp.float32)
    norm_scale = lax.rsqrt(lax.optimization_barrier(jnp.mean(residual_sum * residual_sum, axis=-1, keepdims=True)) + 1e-06)
    moe_in = (residual_sum * norm_scale * norm_gain.astype(jnp.float32)).astype(jnp.bfloat16)
    load_most = N_SEQ * N_EXP * CAP

    def expert_step(carried, scanned):
        gate_w, up_w, down_w, expert_id = scanned
        matches = routes == expert_id
        chosen = jnp.any(matches, axis=1)
        weight_sum = lax.optimization_barrier(jnp.sum(jnp.where(matches, route_weights, 0.0), axis=1))
        position = (jnp.cumsum(chosen.astype(jnp.int32)) - 1).astype(jnp.int32)
        target = jnp.where(chosen, position, load_most).astype(jnp.int32)
        buffer = jnp.zeros((load_most, D), jnp.bfloat16).at[target].set(moe_in, mode='drop')
        gate_proj = jnp.dot(buffer, gate_w, preferred_element_type=jnp.float32)
        up_proj = jnp.dot(buffer, up_w, preferred_element_type=jnp.float32)
        hidden = (jax.nn.silu(gate_proj) * up_proj).astype(jnp.bfloat16)
        result = jnp.dot(hidden, down_w, preferred_element_type=jnp.float32).astype(jnp.bfloat16)
        returned = result[jnp.clip(position, 0, load_most - 1).astype(jnp.int32)]
        weight_used = jnp.where(chosen, weight_sum, 0.0)
        return (carried + returned.astype(jnp.float32) * weight_used[:, None], None)
    moe_sum, unused_out = lax.scan(expert_step, jnp.zeros((TOKENS, D), jnp.float32), (w_gate, w_up, w_down, jnp.arange(EXPERTS, dtype=jnp.int32)))
    return (attn_proj, moe_sum.astype(jnp.bfloat16))
```

```python
import math

import jax
import jax.numpy as jnp
from jax import lax
from jax.experimental import pallas as pl
from jax.experimental.pallas import tpu as pltpu
from jax.sharding import PartitionSpec as P

HD = 128
BLOCK = 1024
ROUTE_K = 8


NEG_FILL = -1e30


def pair_partial(query_blk, key_blk, value_blk, own_block):
    inv_root = 1.0 / math.sqrt(query_blk.shape[-1])
    scores = (
        jnp.einsum("qhd,khd->hqk", query_blk, key_blk, preferred_element_type=jnp.float32)
        * inv_root
    )
    length = query_blk.shape[0]
    query_pos = lax.broadcasted_iota(jnp.int32, (length, length), 0)
    key_pos = lax.broadcasted_iota(jnp.int32, (length, length), 1)
    allowed = jnp.logical_or(jnp.logical_not(own_block), key_pos <= query_pos)[None]
    masked = jnp.where(allowed, scores, NEG_FILL)
    row_max = jnp.max(masked, axis=-1)
    weights = jnp.where(allowed, jnp.exp(masked - row_max[..., None]), 0.0)
    amount = jnp.sum(weights, axis=-1)
    mixed_rows = jnp.einsum(
        "hqk,khd->qhd", weights.astype(jnp.bfloat16), value_blk, preferred_element_type=jnp.float32
    )
    block_part = (mixed_rows / jnp.transpose(amount)[..., None]).astype(jnp.bfloat16)
    return (block_part, row_max, amount)


def merge_partial(carried, incoming):
    running_max, running_sum, running_out = carried
    block_part, row_max, amount = incoming
    new_max = jnp.maximum(running_max, row_max)
    old_factor = jnp.exp(running_max - new_max)
    new_factor = jnp.exp(row_max - new_max) * amount
    running_sum = running_sum * old_factor + new_factor
    running_out = (
        running_out * jnp.swapaxes(old_factor, -1, -2)[..., None]
        + block_part.astype(jnp.float32) * jnp.swapaxes(new_factor, -1, -2)[..., None]
    )
    return (new_max, running_sum, running_out)


def finish_attention(carried):
    running_max, running_sum, running_out = carried
    result = running_out / jnp.swapaxes(running_sum, -1, -2)[..., None]
    return result.astype(jnp.bfloat16)


def expert_kernel(n_ff, rows_ref, gate_ref, up_ref, down_ref, out_ref, hidden_ref):
    step = pl.program_id(0)
    n_rows = rows_ref.shape[0]
    ff_tile = gate_ref.shape[2]
    row_tile = 256

    @pl.when(step < n_ff)
    def _():
        @pl.loop(0, n_rows // row_tile)
        def _(i):
            at = pl.ds(pl.multiple_of(i * row_tile, row_tile), row_tile)
            rows = rows_ref[at, :]
            gate = jnp.dot(rows, gate_ref[0], preferred_element_type=jnp.float32)
            up = jnp.dot(rows, up_ref[0], preferred_element_type=jnp.float32)
            hidden = gate / (1.0 + jnp.exp(-gate)) * up
            cols = pl.ds(pl.multiple_of(step * ff_tile, ff_tile), ff_tile)
            hidden_ref[at, cols] = hidden.astype(jnp.bfloat16)

    @pl.when(step >= n_ff)
    def _():
        @pl.loop(0, n_rows // row_tile)
        def _(i):
            at = pl.ds(pl.multiple_of(i * row_tile, row_tile), row_tile)
            out_ref[at, :] = jnp.dot(
                hidden_ref[at, :], down_ref[0], preferred_element_type=jnp.float32
            ).astype(jnp.bfloat16)


def expert_rows(rows, w_gate, w_up, w_down):
    n_rows, width = rows.shape
    ff = w_gate.shape[2]
    ff_tile, out_tile = 256, 512
    n_ff, n_out = ff // ff_tile, width // out_tile

    def ff_at(i):
        return (0, 0, jnp.minimum(i, n_ff - 1))

    def out_at(i):
        return jnp.maximum(i - n_ff, 0)

    return pl.pallas_call(
        lambda *refs: expert_kernel(n_ff, *refs),
        grid=(n_ff + n_out,),
        in_specs=[
            pl.BlockSpec((n_rows, width), lambda i: (0, 0)),
            pl.BlockSpec((1, width, ff_tile), ff_at),
            pl.BlockSpec((1, width, ff_tile), ff_at),
            pl.BlockSpec((1, ff, out_tile), lambda i: (0, 0, out_at(i))),
        ],
        out_specs=pl.BlockSpec((n_rows, out_tile), lambda i: (0, out_at(i))),
        out_shape=jax.ShapeDtypeStruct((n_rows, width), jnp.bfloat16),
        scratch_shapes=[pltpu.VMEM((n_rows, ff), jnp.bfloat16)],
        compiler_params=pltpu.CompilerParams(vmem_limit_bytes=44 * 1024 * 1024),
        cost_estimate=pl.CostEstimate(
            flops=6 * n_rows * width * ff,
            bytes_accessed=2 * (2 * n_rows * width + 3 * width * ff),
            transcendentals=n_rows * ff,
        ),
        name="experts",
    )(rows, w_gate, w_up, w_down)


def slot_tables(routes, route_weights, n_experts, cap):
    n_tok = routes.shape[0]
    expert_ids = lax.broadcasted_iota(jnp.int32, (n_experts, n_tok), 0)
    hit = jnp.zeros((n_experts, n_tok), jnp.bool_)
    weight = jnp.zeros((n_experts, n_tok), jnp.float32)
    for k in range(routes.shape[1]):
        match = routes[:, k][None, :] == expert_ids
        hit = jnp.logical_or(hit, match)
        weight = weight + jnp.where(match, route_weights[:, k][None, :], 0.0)
    ahead = lax.broadcasted_iota(jnp.int32, (n_tok, n_tok), 0) < lax.broadcasted_iota(
        jnp.int32, (n_tok, n_tok), 1
    )
    rank = jnp.dot(
        hit.astype(jnp.bfloat16), ahead.astype(jnp.bfloat16), preferred_element_type=jnp.float32
    ).astype(jnp.int32)
    slot_ids = lax.broadcasted_iota(jnp.int32, (n_experts, cap, n_tok), 1)
    taken = jnp.logical_and(hit[:, None, :], rank[:, None, :] == slot_ids)
    place = taken.astype(jnp.bfloat16).reshape(n_experts * cap, n_tok)
    high = weight.astype(jnp.bfloat16)
    low = (weight - high.astype(jnp.float32)).astype(jnp.bfloat16)
    zero = jnp.zeros((), jnp.bfloat16)
    mix = jnp.concatenate(
        [jnp.where(taken, high[:, None, :], zero), jnp.where(taken, low[:, None, :], zero)], axis=2
    ).reshape(n_experts * cap, 2 * n_tok)
    return place, mix


def per_device(
    queries,
    keys,
    values,
    gates,
    o_proj,
    residual,
    norm_gain,
    routes,
    route_weights,
    w_gate,
    w_up,
    w_down,
):
    n_blocks = gates.shape[0]
    n_local = queries.shape[0] // BLOCK
    heads_here = queries.shape[1] // HD
    first_block = lax.axis_index("seq") * n_local
    block_ids = jnp.arange(n_blocks, dtype=jnp.int32)
    picked = jnp.any(gates[:, :, None] == block_ids[None, None, :], axis=1)
    query_loc = queries.reshape(n_local, BLOCK, heads_here, HD)
    start_state = (
        jnp.full((n_local, heads_here, BLOCK), NEG_FILL, jnp.float32),
        jnp.zeros((n_local, heads_here, BLOCK), jnp.float32),
        jnp.zeros((n_local, BLOCK, heads_here, HD), jnp.float32),
    )
    key_piece = lax.all_gather(keys, "seq", axis=0, tiled=True)
    value_piece = lax.all_gather(values, "seq", axis=0, tiled=True)
    block_count = key_piece.shape[0] // BLOCK
    key_blocks = key_piece.reshape(block_count, BLOCK, heads_here, HD)
    value_blocks = value_piece.reshape(block_count, BLOCK, heads_here, HD)

    def visit(inner_state, scanned):
        key_blk, value_blk, offset = scanned
        key_block_id = offset
        local_id = 0
        query_block_id = first_block + local_id
        current = tuple((member[local_id] for member in inner_state))

        def attend(
            held_state,
            local_id=local_id,
            key_blk=key_blk,
            value_blk=value_blk,
            key_block_id=key_block_id,
            query_block_id=query_block_id,
        ):
            return merge_partial(
                held_state,
                pair_partial(
                    query_loc[local_id], key_blk, value_blk, key_block_id == query_block_id
                ),
            )

        updated = [
            lax.cond(
                picked[query_block_id, key_block_id], attend, lambda held_state: held_state, current
            )
        ]
        stacked = tuple(
            (jnp.stack([entry[member_id] for entry in updated]) for member_id in range(3))
        )
        return (stacked, None)

    folded, unused_out = lax.scan(
        visit, start_state, (key_blocks, value_blocks, jnp.arange(block_count, dtype=jnp.int32))
    )
    attn = finish_attention(folded).reshape(n_local * BLOCK, heads_here * HD)
    tok_moe = residual.shape[0]
    summed = lax.psum_scatter(
        jnp.dot(attn, o_proj, preferred_element_type=jnp.float32).astype(jnp.bfloat16),
        "exp",
        scatter_dimension=0,
        tiled=True,
    )
    residual_sum = residual.astype(jnp.float32) + summed.astype(jnp.float32)
    norm_scale = lax.rsqrt(jnp.mean(residual_sum * residual_sum, axis=-1, keepdims=True) + 1e-06)
    moe_in = (residual_sum * norm_scale * norm_gain).astype(jnp.bfloat16)
    width = moe_in.shape[1]
    n_experts = w_gate.shape[0] * lax.axis_size("seq") * lax.axis_size("exp")
    cap = 2 * tok_moe * ROUTE_K // n_experts
    place, mix = slot_tables(routes, route_weights, n_experts, cap)
    senders = jnp.dot(place, moe_in, preferred_element_type=jnp.float32).astype(jnp.bfloat16)
    received = lax.all_to_all(
        senders.reshape(n_experts, cap, width),
        ("seq", "exp"),
        split_axis=0,
        concat_axis=0,
        tiled=True,
    )
    produced = expert_rows(received.reshape(n_experts * cap, width), w_gate, w_up, w_down)
    returned = lax.all_to_all(
        produced.reshape(n_experts, cap, width),
        ("seq", "exp"),
        split_axis=0,
        concat_axis=0,
        tiled=True,
    )
    halves = lax.dot_general(
        mix,
        returned.reshape(n_experts * cap, width),
        (((0,), (0,)), ((), ())),
        preferred_element_type=jnp.float32,
    )
    moe_out = (halves[:tok_moe] + halves[tok_moe:]).astype(jnp.bfloat16)
    return (summed, moe_out)


def solution(mesh):
    in_specs = (
        P("seq", "exp"),
        P("seq", "exp"),
        P("seq", "exp"),
        P(),
        P("exp", None),
        P(("seq", "exp"), None),
        P(),
        P(("seq", "exp"), None),
        P(("seq", "exp"), None),
        P(("seq", "exp"), None, None),
        P(("seq", "exp"), None, None),
        P(("seq", "exp"), None, None),
    )
    out_specs = (P(("seq", "exp"), None), P(("seq", "exp"), None))
    return jax.shard_map(
        per_device, mesh=mesh, in_specs=in_specs, out_specs=out_specs, check_vma=False
    )
```

```python
import math

import jax
import jax.numpy as jnp
from jax import lax
from jax.experimental import pallas as pl
from jax.experimental.pallas import tpu as pltpu
from jax.sharding import PartitionSpec as P

HD = 128
BLOCK = 1024
ROUTE_K = 8


NEG_FILL = -1e30
SCALE = math.log2(math.e) / math.sqrt(HD)
Q_TILE = 256
CORES = 2
SIDE = 4


def dot_t(a, b):
    return lax.dot_general(a, b, (((1,), (1,)), ((), ())), preferred_element_type=jnp.float32)


def own_kernel(q_ref, k_ref, v_ref, top_ref, sum_ref, acc_ref):
    for i in range(q_ref.shape[0] // Q_TILE):
        at = pl.ds(i * Q_TILE, Q_TILE)
        seen = pl.ds(0, (i + 1) * Q_TILE)
        scores = dot_t(q_ref[at, :], k_ref[seen, :])
        query_pos = lax.broadcasted_iota(jnp.int32, scores.shape, 0) + i * Q_TILE
        key_pos = lax.broadcasted_iota(jnp.int32, scores.shape, 1)
        scores = jnp.where(key_pos <= query_pos, scores, NEG_FILL)
        top = jnp.max(scores, axis=1, keepdims=True)
        weights = jnp.exp2((scores - top) * SCALE)
        top_ref[at, :] = jnp.broadcast_to(top, (Q_TILE, HD))
        sum_ref[at, :] = jnp.broadcast_to(jnp.sum(weights, axis=1, keepdims=True), (Q_TILE, HD))
        acc_ref[at, :] = jnp.dot(
            weights.astype(jnp.bfloat16), v_ref[seen, :], preferred_element_type=jnp.float32
        )


def attend_own(queries, keys, values):
    n, width = queries.shape
    spec = pl.BlockSpec((n, HD), lambda h: (0, h))
    state = jax.ShapeDtypeStruct((n, width), jnp.float32)
    return pl.pallas_call(
        own_kernel,
        grid=(width // HD,),
        in_specs=[spec] * 3,
        out_specs=[spec] * 3,
        out_shape=[state] * 3,
        compiler_params=pltpu.CompilerParams(vmem_limit_bytes=32 * 1024 * 1024),
        cost_estimate=pl.CostEstimate(
            flops=8 * n * n * width, bytes_accessed=18 * n * width, transcendentals=n * n
        ),
        name="attend_own",
    )(queries, keys, values)


def far_kernel(code_ref, q_ref, top_ref, sum_ref, acc_ref, *refs):
    near, swapped, out_ref = refs[:-6], refs[-6], refs[-5]
    held, tops, sums, accs = refs[-4:]
    tops[...] = top_ref[...]
    sums[...] = sum_ref[...]
    accs[...] = acc_ref[...]
    for j in range(swapped.shape[0]):
        code = code_ref[j]
        for s in range(len(near)):

            @pl.when(code == s + 1)
            def _(s=s):
                held[...] = near[s][...]

        @pl.when(code == len(near) + 1)
        def _(j=j):
            held[...] = swapped[j]

        @pl.when(code > 0)
        def _():
            for i in range(q_ref.shape[0] // Q_TILE):
                at = pl.ds(i * Q_TILE, Q_TILE)
                scores = dot_t(q_ref[at, :], held[:, :HD])
                old = tops[at, :]
                top = jnp.maximum(old, jnp.max(scores, axis=1, keepdims=True))
                weights = jnp.exp2((scores - top[:, :1]) * SCALE)
                fade = jnp.exp2((old - top) * SCALE)
                tops[at, :] = top
                sums[at, :] = sums[at, :] * fade + jnp.sum(weights, axis=1, keepdims=True)
                accs[at, :] = accs[at, :] * fade + jnp.dot(
                    weights.astype(jnp.bfloat16), held[:, HD:], preferred_element_type=jnp.float32
                )

    out_ref[...] = (accs[...] / sums[...]).astype(jnp.bfloat16)


def attend_far(codes, queries, state, near, swapped, head):
    n = queries.shape[0]
    spec = pl.BlockSpec((n, HD), lambda i: (0, head))
    block = pl.BlockSpec((n, 2 * HD), lambda i: (0, 0))
    return pl.pallas_call(
        far_kernel,
        grid=(1,),
        in_specs=[pl.BlockSpec(memory_space=pltpu.SMEM)]
        + [spec] * 4
        + [block] * len(near)
        + [pl.BlockSpec(swapped.shape, lambda i: (0, 0, 0))],
        out_specs=pl.BlockSpec((n, HD), lambda i: (0, 0)),
        out_shape=jax.ShapeDtypeStruct((n, HD), jnp.bfloat16),
        scratch_shapes=[pltpu.VMEM((n, 2 * HD), jnp.bfloat16)]
        + [pltpu.VMEM((n, HD), jnp.float32)] * 3,
        compiler_params=pltpu.CompilerParams(vmem_limit_bytes=40 * 1024 * 1024),
        cost_estimate=pl.CostEstimate(
            flops=16 * n * n * HD, bytes_accessed=24 * n * HD, transcendentals=2 * n * n
        ),
        name="attend_far",
    )(codes, queries, *state, *near, swapped)


def project_kernel(n, *refs):
    out_ref = refs[-1]
    total = jnp.dot(refs[0][...], refs[n][...], preferred_element_type=jnp.float32)
    for i in range(1, n):
        total += jnp.dot(refs[i][...], refs[n + i][...], preferred_element_type=jnp.float32)
    out_ref[...] = total.astype(jnp.bfloat16)


def project(rows, weights):
    n = len(rows)
    n_rows, depth = rows[0].shape
    width = weights[0].shape[1]
    tile = width // 2
    return pl.pallas_call(
        lambda *refs: project_kernel(n, *refs),
        grid=(width // tile,),
        in_specs=[pl.BlockSpec((n_rows, depth), lambda i: (0, 0))] * n
        + [pl.BlockSpec((depth, tile), lambda i: (0, i))] * n,
        out_specs=pl.BlockSpec((n_rows, tile), lambda i: (0, i)),
        out_shape=jax.ShapeDtypeStruct((n_rows, width), jnp.bfloat16),
        compiler_params=pltpu.CompilerParams(vmem_limit_bytes=32 * 1024 * 1024),
        cost_estimate=pl.CostEstimate(
            flops=2 * n * n_rows * depth * width,
            bytes_accessed=2 * n * (n_rows * depth + depth * width) + 2 * n_rows * width,
            transcendentals=0,
        ),
        name="project",
    )(*rows, *weights)


def chip_perm(far):
    return [
        (z * CORES + c, (z + far) * CORES + c) for z in range(SIDE - far) for c in range(CORES)
    ]


def ring_x(array, far):
    perm = [(x * SIDE + y, (x + far) % SIDE * SIDE + y) for x in range(SIDE) for y in range(SIDE)]
    return lax.ppermute(array, "exp", perm)


def ring_y(array, far):
    perm = [(x * SIDE + y, x * SIDE + (y + far) % SIDE) for x in range(SIDE) for y in range(SIDE)]
    return lax.ppermute(array, "exp", perm)


def swap_cores(array):
    perm = [(i, i ^ 1) for i in range(SIDE * CORES)]
    return lax.ppermute(array, "seq", perm)


def attend(queries, keys, values, gates):
    me = lax.axis_index("seq")
    chip, core = me // CORES, me % CORES
    wanted = gates[me, 1:]
    codes = jnp.where(
        wanted == me, 0, jnp.where(wanted % CORES == core, chip - wanted // CORES, SIDE)
    ).astype(jnp.int32)
    partner_far = chip - gates[me ^ 1, 1:] // CORES
    state = attend_own(queries, keys, values)
    outs = []
    for head in range(queries.shape[1] // HD):
        cols = slice(head * HD, (head + 1) * HD)
        own = jnp.concatenate([keys[:, cols], values[:, cols]], axis=1)
        near = [lax.ppermute(own, "seq", chip_perm(far)) for far in range(1, SIDE)]
        asked = []
        for j in range(wanted.shape[0]):
            block = own
            for far in range(1, SIDE):
                block = jnp.where(partner_far[j] == far, near[far - 1], block)
            asked.append(block)
        swapped = swap_cores(jnp.stack(asked))
        outs.append(attend_far(codes, queries, state, near, swapped, head))
    return jnp.concatenate(outs, axis=1)


def projected(attn, o_proj, tok_moe):
    at = lax.axis_index("exp")
    x, y = at // SIDE, at % SIDE
    half = o_proj.shape[1] // 2
    width = attn.shape[1]
    grid = attn.reshape(SIDE, SIDE, tok_moe, width)
    out = []
    for ring, other, mine, theirs, cols, axis in (
        (ring_x, ring_y, x, y, slice(0, half), 0),
        (ring_y, ring_x, y, x, slice(half, None), 1),
    ):
        shard = o_proj[:, cols]
        weights = [shard] + [ring(shard, far) for far in range(1, SIDE)]
        rows = []
        for far in range(SIDE):
            piece = lax.dynamic_index_in_dim(grid, (mine + far) % SIDE, axis, keepdims=False)
            piece = piece.reshape(SIDE * tok_moe, width)
            rows.append(ring(piece, far) if far else piece)
        partial = project(rows, weights).reshape(SIDE, tok_moe, half)
        total = lax.dynamic_index_in_dim(partial, theirs, 0, keepdims=False).astype(jnp.float32)
        for far in range(1, SIDE):
            piece = lax.dynamic_index_in_dim(partial, (theirs + far) % SIDE, 0, keepdims=False)
            total = total + other(piece, far).astype(jnp.float32)
        out.append(total.astype(jnp.bfloat16))
    return jnp.concatenate(out, axis=1)


def expert_kernel(n_ff, rows_ref, gate_ref, up_ref, down_ref, out_ref, hidden_ref):
    step = pl.program_id(0)
    ff_tile = gate_ref.shape[2]

    @pl.when(step < n_ff)
    def _():
        rows = rows_ref[...]
        gate = jnp.dot(rows, gate_ref[0], preferred_element_type=jnp.float32)
        up = jnp.dot(rows, up_ref[0], preferred_element_type=jnp.float32)
        hidden = gate / (1.0 + jnp.exp(-gate)) * up
        cols = pl.ds(pl.multiple_of(step * ff_tile, ff_tile), ff_tile)
        hidden_ref[:, cols] = hidden.astype(jnp.bfloat16)

    @pl.when(step >= n_ff)
    def _():
        out_ref[...] = jnp.dot(
            hidden_ref[...], down_ref[0], preferred_element_type=jnp.float32
        ).astype(jnp.bfloat16)


def expert_rows(rows, w_gate, w_up, w_down):
    n_rows, width = rows.shape
    ff = w_gate.shape[2]
    ff_tile, out_tile = 256, 512
    n_ff, n_out = ff // ff_tile, width // out_tile

    def ff_at(i):
        return (0, 0, jnp.minimum(i, n_ff - 1))

    def out_at(i):
        return jnp.maximum(i - n_ff, 0)

    return pl.pallas_call(
        lambda *refs: expert_kernel(n_ff, *refs),
        grid=(n_ff + n_out,),
        in_specs=[
            pl.BlockSpec((n_rows, width), lambda i: (0, 0)),
            pl.BlockSpec((1, width, ff_tile), ff_at),
            pl.BlockSpec((1, width, ff_tile), ff_at),
            pl.BlockSpec((1, ff, out_tile), lambda i: (0, 0, out_at(i))),
        ],
        out_specs=pl.BlockSpec((n_rows, out_tile), lambda i: (0, out_at(i))),
        out_shape=jax.ShapeDtypeStruct((n_rows, width), jnp.bfloat16),
        scratch_shapes=[pltpu.VMEM((n_rows, ff), jnp.bfloat16)],
        compiler_params=pltpu.CompilerParams(vmem_limit_bytes=44 * 1024 * 1024),
        cost_estimate=pl.CostEstimate(
            flops=6 * n_rows * width * ff,
            bytes_accessed=2 * (2 * n_rows * width + 3 * width * ff),
            transcendentals=n_rows * ff,
        ),
        name="experts",
    )(rows, w_gate, w_up, w_down)


def slot_tables(routes, route_weights, n_experts, cap):
    n_tok = routes.shape[0]
    expert_ids = lax.broadcasted_iota(jnp.int32, (n_experts, n_tok), 0)
    hit = jnp.zeros((n_experts, n_tok), jnp.bool_)
    weight = jnp.zeros((n_experts, n_tok), jnp.float32)
    for k in range(routes.shape[1]):
        match = routes[:, k][None, :] == expert_ids
        hit = jnp.logical_or(hit, match)
        weight = weight + jnp.where(match, route_weights[:, k][None, :], 0.0)
    ahead = lax.broadcasted_iota(jnp.int32, (n_tok, n_tok), 0) < lax.broadcasted_iota(
        jnp.int32, (n_tok, n_tok), 1
    )
    rank = jnp.dot(
        hit.astype(jnp.bfloat16), ahead.astype(jnp.bfloat16), preferred_element_type=jnp.float32
    ).astype(jnp.int32)
    slot_ids = lax.broadcasted_iota(jnp.int32, (n_experts, cap, n_tok), 1)
    taken = jnp.logical_and(hit[:, None, :], rank[:, None, :] == slot_ids)
    place = taken.astype(jnp.bfloat16).reshape(n_experts * cap, n_tok)
    high = weight.astype(jnp.bfloat16)
    low = (weight - high.astype(jnp.float32)).astype(jnp.bfloat16)
    zero = jnp.zeros((), jnp.bfloat16)
    mix = jnp.concatenate(
        [jnp.where(taken, high[:, None, :], zero), jnp.where(taken, low[:, None, :], zero)], axis=2
    ).reshape(n_experts * cap, 2 * n_tok)
    return place, mix


def per_device(
    queries,
    keys,
    values,
    gates,
    o_proj,
    residual,
    norm_gain,
    routes,
    route_weights,
    w_gate,
    w_up,
    w_down,
):
    tok_moe = residual.shape[0]
    summed = projected(attend(queries, keys, values, gates), o_proj, tok_moe)
    residual_sum = residual.astype(jnp.float32) + summed.astype(jnp.float32)
    norm_scale = lax.rsqrt(jnp.mean(residual_sum * residual_sum, axis=-1, keepdims=True) + 1e-06)
    moe_in = (residual_sum * norm_scale * norm_gain).astype(jnp.bfloat16)
    width = moe_in.shape[1]
    n_experts = w_gate.shape[0] * lax.axis_size("seq") * lax.axis_size("exp")
    cap = 2 * tok_moe * ROUTE_K // n_experts
    place, mix = slot_tables(routes, route_weights, n_experts, cap)
    senders = jnp.dot(place, moe_in, preferred_element_type=jnp.float32).astype(jnp.bfloat16)
    received = lax.all_to_all(
        senders.reshape(n_experts, cap, width),
        ("seq", "exp"),
        split_axis=0,
        concat_axis=0,
        tiled=True,
    )
    produced = expert_rows(received.reshape(n_experts * cap, width), w_gate, w_up, w_down)
    returned = lax.all_to_all(
        produced.reshape(n_experts, cap, width),
        ("seq", "exp"),
        split_axis=0,
        concat_axis=0,
        tiled=True,
    )
    halves = lax.dot_general(
        mix,
        returned.reshape(n_experts * cap, width),
        (((0,), (0,)), ((), ())),
        preferred_element_type=jnp.float32,
    )
    moe_out = (halves[:tok_moe] + halves[tok_moe:]).astype(jnp.bfloat16)
    return (summed, moe_out)


def solution(mesh):
    in_specs = (
        P("seq", "exp"),
        P("seq", "exp"),
        P("seq", "exp"),
        P(),
        P("exp", None),
        P(("seq", "exp"), None),
        P(),
        P(("seq", "exp"), None),
        P(("seq", "exp"), None),
        P(("seq", "exp"), None, None),
        P(("seq", "exp"), None, None),
        P(("seq", "exp"), None, None),
    )
    out_specs = (P(("seq", "exp"), None), P(("seq", "exp"), None))
    return jax.shard_map(
        per_device, mesh=mesh, in_specs=in_specs, out_specs=out_specs, check_vma=False
    )
```

```python
import math

import jax
import jax.numpy as jnp
from jax import lax
from jax.experimental import pallas as pl
from jax.experimental.pallas import tpu as pltpu
from jax.sharding import PartitionSpec as P

HD = 128
BLOCK = 1024
ROUTE_K = 8


NEG_FILL = -1e30
SCALE = math.log2(math.e) / math.sqrt(HD)
Q_TILE = 128
CORES = 2
SIDE = 4


def dot_t(a, b):
    return lax.dot_general(a, b, (((1,), (1,)), ((), ())), preferred_element_type=jnp.float32)


def mix_values(weights, values):
    wide = jnp.concatenate([values, jnp.ones_like(values)], axis=1)
    both = jnp.dot(weights.astype(jnp.bfloat16), wide, preferred_element_type=jnp.float32)
    return both[:, :HD], both[:, HD:]


def attend_kernel(code_ref, q_ref, own_ref, *refs):
    near, swapped, out_ref = refs[:-6], refs[-6], refs[-5]
    held, tops, sums, accs = refs[-4:]
    n_tiles = q_ref.shape[0] // Q_TILE
    for i in range(n_tiles):
        at = pl.ds(i * Q_TILE, Q_TILE)
        seen = pl.ds(0, (i + 1) * Q_TILE)
        scores = dot_t(q_ref[at, :], own_ref[seen, :HD])
        query_pos = lax.broadcasted_iota(jnp.int32, scores.shape, 0) + i * Q_TILE
        key_pos = lax.broadcasted_iota(jnp.int32, scores.shape, 1)
        scores = jnp.where(key_pos <= query_pos, scores, NEG_FILL)
        top = jnp.max(scores, axis=1, keepdims=True)
        weights = jnp.exp2((scores - top) * SCALE)
        acc, amount = mix_values(weights, own_ref[seen, HD:])
        tops[at, :] = jnp.broadcast_to(top, (Q_TILE, HD))
        sums[at, :] = amount
        accs[at, :] = acc
    for j in range(swapped.shape[0]):
        code = code_ref[j]
        for s in range(len(near)):

            @pl.when(code == s + 1)
            def _(s=s):
                held[...] = near[s][...]

        @pl.when(code == len(near) + 1)
        def _(j=j):
            held[...] = swapped[j]

        @pl.when(code > 0)
        def _():
            for i in range(n_tiles):
                at = pl.ds(i * Q_TILE, Q_TILE)
                scores = dot_t(q_ref[at, :], held[:, :HD])
                old = tops[at, :]
                top = jnp.maximum(old, jnp.max(scores, axis=1, keepdims=True))
                weights = jnp.exp2((scores - top[:, :1]) * SCALE)
                fade = jnp.exp2((old - top) * SCALE)
                acc, amount = mix_values(weights, held[:, HD:])
                tops[at, :] = top
                sums[at, :] = sums[at, :] * fade + amount
                accs[at, :] = accs[at, :] * fade + acc

    out_ref[...] = (accs[...] / sums[...]).astype(jnp.bfloat16)


def attend_head(codes, queries, own, near, swapped, head, before):
    n = queries.shape[0]
    block = pl.BlockSpec((n, 2 * HD), lambda i: (0, 0))
    extra = [] if before is None else [before]
    return pl.pallas_call(
        lambda *refs: attend_kernel(*refs[len(extra) :]),
        grid=(1,),
        in_specs=[pl.BlockSpec(memory_space=pl.ANY)] * len(extra)
        + [
            pl.BlockSpec(memory_space=pltpu.SMEM),
            pl.BlockSpec((n, HD), lambda i: (0, head)),
        ]
        + [block] * (1 + len(near))
        + [pl.BlockSpec(swapped.shape, lambda i: (0, 0, 0))],
        out_specs=pl.BlockSpec((n, HD), lambda i: (0, head)),
        out_shape=jax.ShapeDtypeStruct(queries.shape, jnp.bfloat16),
        input_output_aliases={0: 0} if extra else {},
        scratch_shapes=[pltpu.VMEM((n, 2 * HD), jnp.bfloat16)]
        + [pltpu.VMEM((n, HD), jnp.float32)] * 3,
        compiler_params=pltpu.CompilerParams(vmem_limit_bytes=60 * 1024 * 1024),
        cost_estimate=pl.CostEstimate(
            flops=64 * n * n * HD, bytes_accessed=14 * n * HD, transcendentals=2 * n * n
        ),
        name="attend",
    )(*extra, codes, queries, own, *near, swapped)


def project_kernel(core_ref, *refs):
    rows, own, mine, theirs, out_ref = refs[:4], refs[4], refs[5:8], refs[8:11], refs[11]
    core = core_ref[0]
    first = pl.ds(pl.multiple_of(core * HD, HD), HD)
    second = pl.ds(pl.multiple_of((1 - core) * HD, HD), HD)
    total = jnp.dot(rows[0][...], own[...], preferred_element_type=jnp.float32)
    for row, left, right in zip(rows[1:], mine, theirs):
        total += jnp.dot(
            jnp.concatenate([row[:, first], row[:, second]], axis=1),
            jnp.concatenate([left[...], right[...]], axis=0),
            preferred_element_type=jnp.float32,
        )
    out_ref[...] = total.astype(jnp.bfloat16)


def project(core, rows, own, mine, theirs):
    n = len(mine)
    n_rows, depth = rows[0].shape
    width, tile = own.shape[1], 896
    return pl.pallas_call(
        project_kernel,
        grid=(width // tile,),
        in_specs=[pl.BlockSpec(memory_space=pltpu.SMEM)]
        + [pl.BlockSpec((n_rows, depth), lambda i: (0, 0))] * (1 + n)
        + [pl.BlockSpec((depth, tile), lambda i: (0, i))]
        + [pl.BlockSpec((HD, tile), lambda i: (0, i))] * n
        + [pl.BlockSpec((HD, tile), lambda i, k=k: (k, i)) for k in range(n)],
        out_specs=pl.BlockSpec((n_rows, tile), lambda i: (0, i)),
        out_shape=jax.ShapeDtypeStruct((n_rows, width), jnp.bfloat16),
        compiler_params=pltpu.CompilerParams(vmem_limit_bytes=32 * 1024 * 1024),
        cost_estimate=pl.CostEstimate(
            flops=6 * n * n_rows * depth * width,
            bytes_accessed=2 * n * (n_rows * depth + depth * width) + 2 * n_rows * width,
            transcendentals=0,
        ),
        name="project",
    )(core, *rows, own, *mine, *([theirs] * n))


def chip_perm(far):
    return [
        (z * CORES + c, (z + far) * CORES + c) for z in range(SIDE - far) for c in range(CORES)
    ]


def ring_x(array, far):
    perm = [(x * SIDE + y, (x + far) % SIDE * SIDE + y) for x in range(SIDE) for y in range(SIDE)]
    return lax.ppermute(array, "exp", perm)


def ring_y(array, far):
    perm = [(x * SIDE + y, x * SIDE + (y + far) % SIDE) for x in range(SIDE) for y in range(SIDE)]
    return lax.ppermute(array, "exp", perm)


def swap_cores(array):
    perm = [(i, i ^ 1) for i in range(SIDE * CORES)]
    return lax.ppermute(array, "seq", perm)


def after(array, *earlier):
    return lax.optimization_barrier((array, *earlier))[0]


def attend(queries, keys, values, gates, first_shards, last_shard):
    me = lax.axis_index("seq")
    chip, core = me // CORES, me % CORES
    wanted = gates[me, 1:]
    codes = jnp.where(
        wanted == me, 0, jnp.where(wanted % CORES == core, chip - wanted // CORES, SIDE)
    ).astype(jnp.int32)
    partner_far = (chip - gates[me ^ 1, 1:] // CORES)[:, None, None]
    owns = []
    for head in range(queries.shape[1] // HD):
        cols = slice(head * HD, (head + 1) * HD)
        owns.append(jnp.concatenate([keys[:, cols], values[:, cols]], axis=1))
    attn, near = None, None
    for head, own in enumerate(owns):
        if head == 0:
            near = [lax.ppermute(own, "seq", chip_perm(far)) for far in range(1, SIDE)]
            shards = first_shards(own)
            later = [after(own, shards[0]) for own in owns[1:]]
            near, shards, later = lax.optimization_barrier((near, shards, later))
        else:
            sent = later[head - 1]
            near = [
                lax.ppermute(after(sent, seen), "seq", chip_perm(far))
                for far, seen in enumerate(near, 1)
            ]
            if head == 1:
                shards = shards + [last_shard(shards[0])]
            near, attn, shards = lax.optimization_barrier((near, attn, shards))
        asked = own[None]
        for far in range(1, SIDE):
            asked = jnp.where(partner_far == far, near[far - 1][None], asked)
        swapped = swap_cores(asked)
        attn = attend_head(codes, queries, own, near, swapped, head, attn)
    return attn, [after(shard, swapped) for shard in shards]


def projected(queries, keys, values, gates, o_proj, tok_moe):
    at = lax.axis_index("exp")
    x, y = at // SIDE, at % SIDE
    order = (1, 3, 2)

    core = lax.axis_index("seq") % CORES
    share = (core * HD, 0), (HD, o_proj.shape[1])

    def first_shards(seen):
        part = lax.dynamic_slice(after(o_proj, seen), *share)
        return [ring_x(part, far) for far in order[:2]]

    def last_shard(seen):
        return ring_x(lax.dynamic_slice(after(o_proj, seen), *share), order[2])

    attn, mine = attend(queries, keys, values, gates, first_shards, last_shard)
    theirs = swap_cores(jnp.concatenate(mine, axis=0))
    n_rows, width = attn.shape[0] // SIDE, attn.shape[1]
    rows = []
    for far in (0,) + order:
        piece = lax.dynamic_slice(attn, ((x + far) % SIDE * n_rows, 0), (n_rows, width))
        rows.append(ring_x(piece, far) if far else piece)
    partial = project(core.reshape(1), rows, o_proj, mine, theirs)
    total = None
    for far in (0,) + order:
        start = (y + far) % SIDE * tok_moe
        piece = lax.dynamic_slice(partial, (start, 0), (tok_moe, partial.shape[1]))
        if far:
            piece = ring_y(piece, far)
        piece = piece.astype(jnp.float32)
        total = piece if total is None else total + piece
    return total.astype(jnp.bfloat16)


def expert_kernel(n_ff, rows_ref, gate_ref, up_ref, down_ref, out_ref, hidden_ref):
    step = pl.program_id(0)
    ff_tile = gate_ref.shape[2]

    @pl.when(step < n_ff)
    def _():
        rows = rows_ref[...]
        gate = jnp.dot(rows, gate_ref[0], preferred_element_type=jnp.float32)
        up = jnp.dot(rows, up_ref[0], preferred_element_type=jnp.float32)
        hidden = gate / (1.0 + jnp.exp(-gate)) * up
        cols = pl.ds(pl.multiple_of(step * ff_tile, ff_tile), ff_tile)
        hidden_ref[:, cols] = hidden.astype(jnp.bfloat16)

    @pl.when(step >= n_ff)
    def _():
        out_ref[...] = jnp.dot(
            hidden_ref[...], down_ref[0], preferred_element_type=jnp.float32
        ).astype(jnp.bfloat16)


def expert_rows(rows, w_gate, w_up, w_down):
    n_rows, width = rows.shape
    ff = w_gate.shape[2]
    ff_tile, out_tile = 256, 512
    n_ff, n_out = ff // ff_tile, width // out_tile

    def ff_at(i):
        return (0, 0, jnp.minimum(i, n_ff - 1))

    def out_at(i):
        return jnp.maximum(i - n_ff, 0)

    return pl.pallas_call(
        lambda *refs: expert_kernel(n_ff, *refs),
        grid=(n_ff + n_out,),
        in_specs=[
            pl.BlockSpec(memory_space=pltpu.VMEM),
            pl.BlockSpec((1, width, ff_tile), ff_at),
            pl.BlockSpec((1, width, ff_tile), ff_at),
            pl.BlockSpec((1, ff, out_tile), lambda i: (0, 0, out_at(i))),
        ],
        out_specs=pl.BlockSpec((n_rows, out_tile), lambda i: (0, out_at(i))),
        out_shape=pltpu.HBM((n_rows, width), jnp.bfloat16),
        scratch_shapes=[pltpu.VMEM((n_rows, ff), jnp.bfloat16)],
        compiler_params=pltpu.CompilerParams(vmem_limit_bytes=32 * 1024 * 1024),
        cost_estimate=pl.CostEstimate(
            flops=6 * n_rows * width * ff,
            bytes_accessed=2 * (2 * n_rows * width + 3 * width * ff),
            transcendentals=n_rows * ff,
        ),
        name="experts",
    )(rows, w_gate, w_up, w_down)


def slot_tables(routes, route_weights, n_experts, cap):
    n_tok, n_slots = routes.shape[0], n_experts * cap
    hit = jnp.zeros((n_tok, n_experts), jnp.bool_)
    weight = jnp.zeros((n_tok, n_experts), jnp.float32)
    expert_ids = lax.broadcasted_iota(jnp.int32, (n_tok, n_experts), 1)
    for k in range(routes.shape[1]):
        match = routes[:, k : k + 1] == expert_ids
        hit = jnp.logical_or(hit, match)
        weight = weight + jnp.where(match, route_weights[:, k : k + 1], 0.0)
    square = (n_tok, n_tok)
    ahead = lax.broadcasted_iota(jnp.int32, square, 0) > lax.broadcasted_iota(jnp.int32, square, 1)
    rank = jnp.dot(
        ahead.astype(jnp.bfloat16), hit.astype(jnp.bfloat16), preferred_element_type=jnp.float32
    )
    place = jnp.where(hit, rank, float(2 * n_tok)).astype(jnp.bfloat16)
    high = weight.astype(jnp.bfloat16)
    low = (weight - high.astype(jnp.float32)).astype(jnp.bfloat16)
    spread = lax.broadcasted_iota(jnp.int32, (n_experts, n_slots), 0) == (
        lax.broadcasted_iota(jnp.int32, (n_experts, n_slots), 1) // cap
    )
    wide = jnp.dot(
        jnp.concatenate([place, high, low], axis=0),
        spread.astype(jnp.bfloat16),
        preferred_element_type=jnp.float32,
    )
    slot_ids = lax.broadcasted_iota(jnp.int32, (n_tok, n_slots), 1) % cap
    taken = wide[:n_tok] == slot_ids.astype(jnp.float32)
    pick = taken.astype(jnp.bfloat16)
    mix = jnp.where(jnp.concatenate([taken, taken], axis=0), wide[n_tok:], 0.0)
    return pick.T, mix.astype(jnp.bfloat16)


def combine_kernel(mix_ref, rows_ref, out_ref):
    n_tok, tile = out_ref.shape
    cols = pl.ds(pl.multiple_of(pl.program_id(0) * tile, tile), tile)
    halves = jnp.dot(mix_ref[...], rows_ref[:, cols], preferred_element_type=jnp.float32)
    out_ref[...] = (halves[:n_tok] + halves[n_tok:]).astype(jnp.bfloat16)


def combine(mix, rows):
    n_rows, width = rows.shape
    n_tok, tile = mix.shape[0] // 2, 896
    return pl.pallas_call(
        combine_kernel,
        grid=(width // tile,),
        in_specs=[pl.BlockSpec(memory_space=pltpu.VMEM)] * 2,
        out_specs=pl.BlockSpec((n_tok, tile), lambda i: (0, i)),
        out_shape=jax.ShapeDtypeStruct((n_tok, width), jnp.bfloat16),
        compiler_params=pltpu.CompilerParams(vmem_limit_bytes=24 * 1024 * 1024),
        cost_estimate=pl.CostEstimate(
            flops=4 * n_tok * n_rows * width, bytes_accessed=2 * n_rows * width, transcendentals=0
        ),
        name="combine",
    )(mix, rows)


def per_device(
    queries,
    keys,
    values,
    gates,
    o_proj,
    residual,
    norm_gain,
    routes,
    route_weights,
    w_gate,
    w_up,
    w_down,
):
    tok_moe = residual.shape[0]
    summed = projected(queries, keys, values, gates, o_proj, tok_moe)
    residual_sum = residual.astype(jnp.float32) + summed.astype(jnp.float32)
    norm_scale = lax.rsqrt(jnp.mean(residual_sum * residual_sum, axis=-1, keepdims=True) + 1e-06)
    moe_in = (residual_sum * norm_scale * norm_gain).astype(jnp.bfloat16)
    width = moe_in.shape[1]
    n_experts = w_gate.shape[0] * lax.axis_size("seq") * lax.axis_size("exp")
    cap = 2 * tok_moe * ROUTE_K // n_experts
    place, mix = slot_tables(routes, route_weights, n_experts, cap)
    senders = jnp.dot(place, moe_in, preferred_element_type=jnp.float32).astype(jnp.bfloat16)
    received = lax.all_to_all(
        senders.reshape(n_experts, cap, width),
        ("seq", "exp"),
        split_axis=0,
        concat_axis=0,
        tiled=True,
    )
    produced = expert_rows(received.reshape(n_experts * cap, width), w_gate, w_up, w_down)
    returned = lax.all_to_all(
        produced.reshape(n_experts, cap, width),
        ("seq", "exp"),
        split_axis=0,
        concat_axis=0,
        tiled=True,
    )
    moe_out = combine(mix, returned.reshape(n_experts * cap, width))
    return (summed, moe_out)


def solution(mesh):
    in_specs = (
        P("seq", "exp"),
        P("seq", "exp"),
        P("seq", "exp"),
        P(),
        P("exp", None),
        P(("seq", "exp"), None),
        P(),
        P(("seq", "exp"), None),
        P(("seq", "exp"), None),
        P(("seq", "exp"), None, None),
        P(("seq", "exp"), None, None),
        P(("seq", "exp"), None, None),
    )
    out_specs = (P(("seq", "exp"), None), P(("seq", "exp"), None))
    return jax.shard_map(
        per_device, mesh=mesh, in_specs=in_specs, out_specs=out_specs, check_vma=False
    )
```

```python
import math

import jax
import jax.numpy as jnp
from jax import lax
from jax.experimental import pallas as pl
from jax.experimental.pallas import tpu as pltpu
from jax.sharding import PartitionSpec as P

HD = 128
BLOCK = 1024
ROUTE_K = 8


NEG_FILL = -1e30
SCALE = math.log2(math.e) / math.sqrt(HD)
Q_TILE = 128
CORES = 2
SIDE = 4


def dot_t(a, b):
    return lax.dot_general(a, b, (((1,), (1,)), ((), ())), preferred_element_type=jnp.float32)


def mix_values(weights, values):
    wide = jnp.concatenate([values, jnp.ones_like(values)], axis=1)
    both = jnp.dot(weights.astype(jnp.bfloat16), wide, preferred_element_type=jnp.float32)
    return both[:, :HD], both[:, HD:]


def own_kernel(q_ref, kv_ref, top_ref, sum_ref, acc_ref):
    for i in range(q_ref.shape[0] // Q_TILE):
        at = pl.ds(i * Q_TILE, Q_TILE)
        seen = pl.ds(0, (i + 1) * Q_TILE)
        scores = dot_t(q_ref[at, :], kv_ref[0, seen, :])
        query_pos = lax.broadcasted_iota(jnp.int32, scores.shape, 0) + i * Q_TILE
        key_pos = lax.broadcasted_iota(jnp.int32, scores.shape, 1)
        scores = jnp.where(key_pos <= query_pos, scores, NEG_FILL)
        top = jnp.max(scores, axis=1, keepdims=True)
        weights = jnp.exp2((scores - top) * SCALE)
        acc, amount = mix_values(weights, kv_ref[1, seen, :])
        top_ref[at, :] = jnp.broadcast_to(top, (Q_TILE, HD))
        sum_ref[at, :] = amount
        acc_ref[at, :] = acc


def attend_own(queries, kv):
    n, width = queries.shape
    spec = pl.BlockSpec((n, HD), lambda h: (0, h))
    return pl.pallas_call(
        own_kernel,
        grid=(width // HD,),
        in_specs=[spec, pl.BlockSpec((2, n, HD), lambda h: (0, 0, h))],
        out_specs=[spec] * 3,
        out_shape=[jax.ShapeDtypeStruct((n, width), jnp.float32)] * 3,
        compiler_params=pltpu.CompilerParams(vmem_limit_bytes=60 * 1024 * 1024),
        cost_estimate=pl.CostEstimate(
            flops=8 * n * n * width, bytes_accessed=18 * n * width, transcendentals=n * n
        ),
        name="attend_own",
    )(queries, kv)


def far_kernel(code_ref, q_ref, top_ref, sum_ref, acc_ref, *refs):
    near, swapped, out_ref = refs[:-6], refs[-6], refs[-5]
    held, tops, sums, accs = refs[-4:]
    tops[...] = top_ref[...]
    sums[...] = sum_ref[...]
    accs[...] = acc_ref[...]
    for j in range(swapped.shape[0]):
        code = code_ref[j]
        for s in range(len(near)):

            @pl.when(code == s + 1)
            def _(s=s):
                held[...] = near[s][...]

        @pl.when(code == len(near) + 1)
        def _(j=j):
            held[...] = swapped[j]

        @pl.when(code > 0)
        def _():
            for i in range(q_ref.shape[0] // Q_TILE):
                at = pl.ds(i * Q_TILE, Q_TILE)
                scores = dot_t(q_ref[at, :], held[0])
                old = tops[at, :]
                top = jnp.maximum(old, jnp.max(scores, axis=1, keepdims=True))
                weights = jnp.exp2((scores - top[:, :1]) * SCALE)
                fade = jnp.exp2((old - top) * SCALE)
                acc, amount = mix_values(weights, held[1])
                tops[at, :] = top
                sums[at, :] = sums[at, :] * fade + amount
                accs[at, :] = accs[at, :] * fade + acc

    out_ref[...] = (accs[...] / sums[...]).astype(jnp.bfloat16)


def attend_far(codes, queries, state, near, swapped, head, before):
    n = queries.shape[0]
    spec = pl.BlockSpec((n, HD), lambda i: (0, head))
    extra = [] if before is None else [before]
    return pl.pallas_call(
        lambda *refs: far_kernel(*refs[len(extra) :]),
        grid=(1,),
        in_specs=[pl.BlockSpec(memory_space=pl.ANY)] * len(extra)
        + [pl.BlockSpec(memory_space=pltpu.SMEM)]
        + [spec] * 4
        + [pl.BlockSpec((2, n, HD), lambda i: (0, 0, head))] * len(near)
        + [pl.BlockSpec(swapped.shape, lambda i: (0, 0, 0, 0))],
        out_specs=spec,
        out_shape=jax.ShapeDtypeStruct(queries.shape, jnp.bfloat16),
        input_output_aliases={0: 0} if extra else {},
        scratch_shapes=[pltpu.VMEM((2, n, HD), jnp.bfloat16)]
        + [pltpu.VMEM((n, HD), jnp.float32)] * 3,
        compiler_params=pltpu.CompilerParams(vmem_limit_bytes=60 * 1024 * 1024),
        cost_estimate=pl.CostEstimate(
            flops=48 * n * n * HD, bytes_accessed=24 * n * HD, transcendentals=2 * n * n
        ),
        name="attend_far",
    )(*extra, codes, queries, *state, *near, swapped)


def choose_kernel(far_ref, *refs):
    blocks, out_ref = refs[:-1], refs[-1]
    for j in range(out_ref.shape[0]):
        for far, block in enumerate(blocks):

            @pl.when(far_ref[j] == far)
            def _(j=j, block=block):
                out_ref[j] = block[...]


def choose(fars, blocks, head):
    n = blocks[0].shape[1]
    count = fars.shape[0]
    return pl.pallas_call(
        choose_kernel,
        grid=(1,),
        in_specs=[pl.BlockSpec(memory_space=pltpu.SMEM)]
        + [pl.BlockSpec((2, n, HD), lambda i: (0, 0, head))] * len(blocks),
        out_specs=pl.BlockSpec((count, 2, n, HD), lambda i: (0, 0, 0, 0)),
        out_shape=jax.ShapeDtypeStruct((count, 2, n, HD), jnp.bfloat16),
        compiler_params=pltpu.CompilerParams(vmem_limit_bytes=60 * 1024 * 1024),
        cost_estimate=pl.CostEstimate(flops=0, bytes_accessed=24 * n * HD, transcendentals=0),
        name="choose",
    )(fars, *blocks)


def project_kernel(core_ref, *refs):
    rows, own, mine, theirs, out_ref = refs[:4], refs[4], refs[5:8], refs[8:11], refs[11]
    core = core_ref[0]
    first = pl.ds(pl.multiple_of(core * HD, HD), HD)
    second = pl.ds(pl.multiple_of((1 - core) * HD, HD), HD)
    total = jnp.dot(rows[0][...], own[...], preferred_element_type=jnp.float32)
    for row, left, right in zip(rows[1:], mine, theirs):
        total += jnp.dot(
            jnp.concatenate([row[:, first], row[:, second]], axis=1),
            jnp.concatenate([left[...], right[...]], axis=0),
            preferred_element_type=jnp.float32,
        )
    out_ref[...] = total.astype(jnp.bfloat16)


def project(core, rows, own, mine, theirs):
    n = len(mine)
    n_rows, depth = rows[0].shape
    width, tile = own.shape[1], 896
    return pl.pallas_call(
        project_kernel,
        grid=(width // tile,),
        in_specs=[pl.BlockSpec(memory_space=pltpu.SMEM)]
        + [pl.BlockSpec((n_rows, depth), lambda i: (0, 0))] * (1 + n)
        + [pl.BlockSpec((depth, tile), lambda i: (0, i))]
        + [pl.BlockSpec((HD, tile), lambda i: (0, i))] * n
        + [pl.BlockSpec((HD, tile), lambda i, k=k: (k, i)) for k in (0, 1, 0)],
        out_specs=pl.BlockSpec((n_rows, tile), lambda i: (0, i)),
        out_shape=jax.ShapeDtypeStruct((n_rows, width), jnp.bfloat16),
        compiler_params=pltpu.CompilerParams(vmem_limit_bytes=60 * 1024 * 1024),
        cost_estimate=pl.CostEstimate(
            flops=6 * n * n_rows * depth * width,
            bytes_accessed=2 * n * (n_rows * depth + depth * width) + 2 * n_rows * width,
            transcendentals=0,
        ),
        name="project",
    )(core, *rows, own, *mine, theirs[0], theirs[0], theirs[1])


def chip_perm(far):
    return [
        (z * CORES + c, (z + far) * CORES + c) for z in range(SIDE - far) for c in range(CORES)
    ]


def ring_x(array, far):
    perm = [(x * SIDE + y, (x + far) % SIDE * SIDE + y) for x in range(SIDE) for y in range(SIDE)]
    return lax.ppermute(array, "exp", perm)


def ring_y(array, far):
    perm = [(x * SIDE + y, x * SIDE + (y + far) % SIDE) for x in range(SIDE) for y in range(SIDE)]
    return lax.ppermute(array, "exp", perm)


def swap_cores(array):
    perm = [(i, i ^ 1) for i in range(SIDE * CORES)]
    return lax.ppermute(array, "seq", perm)


def after(array, *earlier):
    return lax.optimization_barrier((array, *earlier))[0]


def attend(queries, keys, values, gates, share, send_share, early):
    me = lax.axis_index("seq")
    chip, core = me // CORES, me % CORES
    wanted = gates[me, 1:]
    codes = jnp.where(
        wanted == me, 0, jnp.where(wanted % CORES == core, chip - wanted // CORES, SIDE)
    ).astype(jnp.int32)
    partner_far = jnp.clip(chip - gates[me ^ 1, 1:] // CORES, 0, SIDE - 1).astype(jnp.int32)
    kv = jnp.stack([keys, values])
    near = [lax.ppermute(kv, "seq", chip_perm(far)) for far in range(1, SIDE)]
    mine = [send_share(share, 1), send_share(share, 3)]
    mine.append(send_share(after(share, *mine), 2))
    state = attend_own(queries, kv)
    joined = jnp.concatenate(mine[:2])
    near, mine, joined, state, early = lax.optimization_barrier(
        (near, mine, joined, state, early)
    )
    heads = range(queries.shape[1] // HD)
    asked = [choose(partner_far, [kv, *near], head) for head in heads]
    swapped = [swap_cores(block) for block in asked]
    theirs = [swap_cores(after(part, asked[-1])) for part in (joined, mine[2])]
    attn = None
    for head in heads:
        attn = attend_far(codes, queries, state, near, swapped[head], head, attn)
    return attn, mine, theirs, early


def projected(queries, keys, values, gates, o_proj, tok_moe, early):
    at = lax.axis_index("exp")
    x, y = at // SIDE, at % SIDE
    order = (1, 3, 2)

    core = lax.axis_index("seq") % CORES
    share = lax.dynamic_slice(o_proj, (core * HD, 0), (HD, o_proj.shape[1]))
    attn, mine, theirs, early = attend(queries, keys, values, gates, share, ring_x, early)
    n_rows, width = attn.shape[0] // SIDE, attn.shape[1]
    rows = []
    for far in (0,) + order:
        piece = lax.dynamic_slice(attn, ((x + far) % SIDE * n_rows, 0), (n_rows, width))
        rows.append(ring_x(piece, far) if far else piece)
    partial = project(core.reshape(1), rows, o_proj, mine, theirs)
    total = None
    for far in (0,) + order:
        start = (y + far) % SIDE * tok_moe
        piece = lax.dynamic_slice(partial, (start, 0), (tok_moe, partial.shape[1]))
        if far:
            piece = ring_y(piece, far)
        piece = piece.astype(jnp.float32)
        total = piece if total is None else total + piece
    return total.astype(jnp.bfloat16), early


def expert_kernel(n_ff, rows_ref, gate_ref, up_ref, down_ref, out_ref, hidden_ref):
    step = pl.program_id(0)
    ff_tile = gate_ref.shape[2]

    @pl.when(step < n_ff)
    def _():
        rows = rows_ref[...]
        gate = jnp.dot(rows, gate_ref[0], preferred_element_type=jnp.float32)
        up = jnp.dot(rows, up_ref[0], preferred_element_type=jnp.float32)
        hidden = gate / (1.0 + jnp.exp(-gate)) * up
        cols = pl.ds(pl.multiple_of(step * ff_tile, ff_tile), ff_tile)
        hidden_ref[:, cols] = hidden.astype(jnp.bfloat16)

    @pl.when(step >= n_ff)
    def _():
        out_ref[...] = jnp.dot(
            hidden_ref[...], down_ref[0], preferred_element_type=jnp.float32
        ).astype(jnp.bfloat16)


def expert_rows(rows, w_gate, w_up, w_down):
    n_rows, width = rows.shape
    ff = w_gate.shape[2]
    ff_tile, out_tile = 256, 512
    n_ff, n_out = ff // ff_tile, width // out_tile

    def ff_at(i):
        return (0, 0, jnp.minimum(i, n_ff - 1))

    def out_at(i):
        return jnp.maximum(i - n_ff, 0)

    return pl.pallas_call(
        lambda *refs: expert_kernel(n_ff, *refs),
        grid=(n_ff + n_out,),
        in_specs=[
            pl.BlockSpec(memory_space=pltpu.VMEM),
            pl.BlockSpec((1, width, ff_tile), ff_at),
            pl.BlockSpec((1, width, ff_tile), ff_at),
            pl.BlockSpec((1, ff, out_tile), lambda i: (0, 0, out_at(i))),
        ],
        out_specs=pl.BlockSpec((n_rows, out_tile), lambda i: (0, out_at(i))),
        out_shape=pltpu.HBM((n_rows, width), jnp.bfloat16),
        scratch_shapes=[pltpu.VMEM((n_rows, ff), jnp.bfloat16)],
        compiler_params=pltpu.CompilerParams(vmem_limit_bytes=32 * 1024 * 1024),
        cost_estimate=pl.CostEstimate(
            flops=6 * n_rows * width * ff,
            bytes_accessed=2 * (2 * n_rows * width + 3 * width * ff),
            transcendentals=n_rows * ff,
        ),
        name="experts",
    )(rows, w_gate, w_up, w_down)


def slot_tables(routes, route_weights, n_experts, cap):
    n_tok, n_slots = routes.shape[0], n_experts * cap
    hit = jnp.zeros((n_tok, n_experts), jnp.bool_)
    weight = jnp.zeros((n_tok, n_experts), jnp.float32)
    expert_ids = lax.broadcasted_iota(jnp.int32, (n_tok, n_experts), 1)
    for k in range(routes.shape[1]):
        match = routes[:, k : k + 1] == expert_ids
        hit = jnp.logical_or(hit, match)
        weight = weight + jnp.where(match, route_weights[:, k : k + 1], 0.0)
    square = (n_tok, n_tok)
    ahead = lax.broadcasted_iota(jnp.int32, square, 0) > lax.broadcasted_iota(jnp.int32, square, 1)
    rank = jnp.dot(
        ahead.astype(jnp.bfloat16), hit.astype(jnp.bfloat16), preferred_element_type=jnp.float32
    )
    place = jnp.where(hit, rank, float(2 * n_tok)).astype(jnp.bfloat16)
    high = weight.astype(jnp.bfloat16)
    low = (weight - high.astype(jnp.float32)).astype(jnp.bfloat16)
    spread = lax.broadcasted_iota(jnp.int32, (n_experts, n_slots), 0) == (
        lax.broadcasted_iota(jnp.int32, (n_experts, n_slots), 1) // cap
    )
    wide = jnp.dot(
        jnp.concatenate([place, high, low], axis=0),
        spread.astype(jnp.bfloat16),
        preferred_element_type=jnp.float32,
    )
    slot_ids = lax.broadcasted_iota(jnp.int32, (n_tok, n_slots), 1) % cap
    taken = wide[:n_tok] == slot_ids.astype(jnp.float32)
    pick = taken.astype(jnp.bfloat16)
    mix = jnp.where(jnp.concatenate([taken, taken], axis=0), wide[n_tok:], 0.0)
    return pick.T, mix.astype(jnp.bfloat16)


def combine_kernel(mix_ref, rows_ref, out_ref):
    n_tok, tile = out_ref.shape
    cols = pl.ds(pl.multiple_of(pl.program_id(0) * tile, tile), tile)
    halves = jnp.dot(mix_ref[...], rows_ref[:, cols], preferred_element_type=jnp.float32)
    out_ref[...] = (halves[:n_tok] + halves[n_tok:]).astype(jnp.bfloat16)


def combine(mix, rows):
    n_rows, width = rows.shape
    n_tok, tile = mix.shape[0] // 2, 896
    return pl.pallas_call(
        combine_kernel,
        grid=(width // tile,),
        in_specs=[pl.BlockSpec(memory_space=pltpu.VMEM)] * 2,
        out_specs=pl.BlockSpec((n_tok, tile), lambda i: (0, i)),
        out_shape=jax.ShapeDtypeStruct((n_tok, width), jnp.bfloat16),
        compiler_params=pltpu.CompilerParams(vmem_limit_bytes=24 * 1024 * 1024),
        cost_estimate=pl.CostEstimate(
            flops=4 * n_tok * n_rows * width, bytes_accessed=2 * n_rows * width, transcendentals=0
        ),
        name="combine",
    )(mix, rows)


def per_device(
    queries,
    keys,
    values,
    gates,
    o_proj,
    residual,
    norm_gain,
    routes,
    route_weights,
    w_gate,
    w_up,
    w_down,
):
    tok_moe, width = residual.shape
    n_experts = w_gate.shape[0] * lax.axis_size("seq") * lax.axis_size("exp")
    cap = 2 * tok_moe * ROUTE_K // n_experts
    tables = slot_tables(routes, route_weights, n_experts, cap)
    summed, (place, mix) = projected(queries, keys, values, gates, o_proj, tok_moe, tables)
    residual_sum = residual.astype(jnp.float32) + summed.astype(jnp.float32)
    norm_scale = lax.rsqrt(jnp.mean(residual_sum * residual_sum, axis=-1, keepdims=True) + 1e-06)
    moe_in = (residual_sum * norm_scale * norm_gain).astype(jnp.bfloat16)
    senders = jnp.dot(place, moe_in, preferred_element_type=jnp.float32).astype(jnp.bfloat16)
    received = lax.all_to_all(
        senders.reshape(n_experts, cap, width),
        ("seq", "exp"),
        split_axis=0,
        concat_axis=0,
        tiled=True,
    )
    produced = expert_rows(received.reshape(n_experts * cap, width), w_gate, w_up, w_down)
    returned = lax.all_to_all(
        produced.reshape(n_experts, cap, width),
        ("seq", "exp"),
        split_axis=0,
        concat_axis=0,
        tiled=True,
    )
    moe_out = combine(mix, returned.reshape(n_experts * cap, width))
    return (summed, moe_out)


def solution(mesh):
    in_specs = (
        P("seq", "exp"),
        P("seq", "exp"),
        P("seq", "exp"),
        P(),
        P("exp", None),
        P(("seq", "exp"), None),
        P(),
        P(("seq", "exp"), None),
        P(("seq", "exp"), None),
        P(("seq", "exp"), None, None),
        P(("seq", "exp"), None, None),
        P(("seq", "exp"), None, None),
    )
    out_specs = (P(("seq", "exp"), None), P(("seq", "exp"), None))
    return jax.shard_map(
        per_device, mesh=mesh, in_specs=in_specs, out_specs=out_specs, check_vma=False
    )
```

```python
import math

import jax
import jax.numpy as jnp
from jax import lax
from jax.experimental import pallas as pl
from jax.experimental.pallas import tpu as pltpu
from jax.sharding import PartitionSpec as P

HD = 128
BLOCK = 1024
ROUTE_K = 8


NEG_FILL = -1e30
SCALE = math.log2(math.e) / math.sqrt(HD)
Q_TILE = 128
CORES = 2
SIDE = 4
ORDER = (1, 3, 2)


def dot_t(a, b):
    return lax.dot_general(a, b, (((1,), (1,)), ((), ())), preferred_element_type=jnp.float32)


def mix_values(weights, values):
    wide = jnp.concatenate([values, jnp.ones_like(values)], axis=1)
    both = jnp.dot(weights.astype(jnp.bfloat16), wide, preferred_element_type=jnp.float32)
    return both[:, :HD], both[:, HD:]


def own_kernel(q_ref, kv_ref, top_ref, sum_ref, acc_ref):
    for i in range(q_ref.shape[0] // Q_TILE):
        at = pl.ds(i * Q_TILE, Q_TILE)
        seen = pl.ds(0, (i + 1) * Q_TILE)
        scores = dot_t(q_ref[at, :], kv_ref[0, seen, :])
        query_pos = lax.broadcasted_iota(jnp.int32, scores.shape, 0) + i * Q_TILE
        key_pos = lax.broadcasted_iota(jnp.int32, scores.shape, 1)
        scores = jnp.where(key_pos <= query_pos, scores, NEG_FILL)
        top = jnp.max(scores, axis=1, keepdims=True)
        weights = jnp.exp2((scores - top) * SCALE)
        acc, amount = mix_values(weights, kv_ref[1, seen, :])
        top_ref[at, :] = jnp.broadcast_to(top, (Q_TILE, HD))
        sum_ref[at, :] = amount
        acc_ref[at, :] = acc


def attend_own(queries, kv):
    n, width = queries.shape
    spec = pl.BlockSpec((n, HD), lambda h: (0, h))
    return pl.pallas_call(
        own_kernel,
        grid=(width // HD,),
        in_specs=[spec, pl.BlockSpec((2, n, HD), lambda h: (0, 0, h))],
        out_specs=[spec] * 3,
        out_shape=[jax.ShapeDtypeStruct((n, width), jnp.float32)] * 3,
        compiler_params=pltpu.CompilerParams(vmem_limit_bytes=60 * 1024 * 1024),
        cost_estimate=pl.CostEstimate(
            flops=8 * n * n * width, bytes_accessed=18 * n * width, transcendentals=n * n
        ),
        name="attend_own",
    )(queries, kv)


def far_kernel(code_ref, q_ref, top_ref, sum_ref, acc_ref, *refs):
    near, swapped, outs = refs[: SIDE - 1], refs[SIDE - 1], refs[SIDE : 2 * SIDE]
    held, tops, sums, accs = refs[-4:]
    tops[...] = top_ref[...]
    sums[...] = sum_ref[...]
    accs[...] = acc_ref[...]
    for j in range(swapped.shape[0]):
        code = code_ref[j]
        for s in range(len(near)):

            @pl.when(code == s + 1)
            def _(s=s):
                held[...] = near[s][...]

        @pl.when(code == len(near) + 1)
        def _(j=j):
            held[...] = swapped[j]

        @pl.when(code > 0)
        def _():
            for i in range(q_ref.shape[0] // Q_TILE):
                at = pl.ds(i * Q_TILE, Q_TILE)
                scores = dot_t(q_ref[at, :], held[0])
                old = tops[at, :]
                top = jnp.maximum(old, jnp.max(scores, axis=1, keepdims=True))
                weights = jnp.exp2((scores - top[:, :1]) * SCALE)
                fade = jnp.exp2((old - top) * SCALE)
                acc, amount = mix_values(weights, held[1])
                tops[at, :] = top
                sums[at, :] = sums[at, :] * fade + amount
                accs[at, :] = accs[at, :] * fade + acc

    n_rows = outs[0].shape[0]
    for far, out_ref in zip((0, *ORDER), outs):
        start = (code_ref[swapped.shape[0]] + far) % SIDE * n_rows
        at = pl.ds(pl.multiple_of(start, n_rows), n_rows)
        out_ref[...] = (accs[at, :] / sums[at, :]).astype(jnp.bfloat16)


def attend_far(codes, queries, state, near, swapped, head, before):
    n, width = queries.shape
    spec = pl.BlockSpec((n, HD), lambda i: (0, head))
    extra = [] if before is None else before
    return pl.pallas_call(
        lambda *refs: far_kernel(*refs[len(extra) :]),
        grid=(1,),
        in_specs=[pl.BlockSpec(memory_space=pl.ANY)] * len(extra)
        + [pl.BlockSpec(memory_space=pltpu.SMEM)]
        + [spec] * 4
        + [pl.BlockSpec((2, n, HD), lambda i: (0, 0, head))] * len(near)
        + [pl.BlockSpec(swapped.shape, lambda i: (0, 0, 0, 0))],
        out_specs=[pl.BlockSpec((n // SIDE, HD), lambda i: (0, head))] * SIDE,
        out_shape=[jax.ShapeDtypeStruct((n // SIDE, width), jnp.bfloat16)] * SIDE,
        input_output_aliases={i: i for i in range(len(extra))},
        scratch_shapes=[pltpu.VMEM((2, n, HD), jnp.bfloat16)]
        + [pltpu.VMEM((n, HD), jnp.float32)] * 3,
        compiler_params=pltpu.CompilerParams(vmem_limit_bytes=60 * 1024 * 1024),
        cost_estimate=pl.CostEstimate(
            flops=48 * n * n * HD, bytes_accessed=24 * n * HD, transcendentals=2 * n * n
        ),
        name="attend_far",
    )(*extra, codes, queries, *state, *near, swapped)


def choose_kernel(far_ref, *refs):
    blocks, out_ref = refs[:-1], refs[-1]
    for j in range(out_ref.shape[0]):
        for far, block in enumerate(blocks):

            @pl.when(far_ref[j] == far)
            def _(j=j, block=block):
                out_ref[j] = block[...]


def choose(fars, blocks, head):
    n = blocks[0].shape[1]
    count = fars.shape[0]
    return pl.pallas_call(
        choose_kernel,
        grid=(1,),
        in_specs=[pl.BlockSpec(memory_space=pltpu.SMEM)]
        + [pl.BlockSpec((2, n, HD), lambda i: (0, 0, head))] * len(blocks),
        out_specs=pl.BlockSpec((count, 2, n, HD), lambda i: (0, 0, 0, 0)),
        out_shape=jax.ShapeDtypeStruct((count, 2, n, HD), jnp.bfloat16),
        compiler_params=pltpu.CompilerParams(vmem_limit_bytes=60 * 1024 * 1024),
        cost_estimate=pl.CostEstimate(flops=0, bytes_accessed=24 * n * HD, transcendentals=0),
        name="choose",
    )(fars, *blocks)


def project_kernel(spot_ref, *refs):
    rows, own, mine, theirs = refs[:4], refs[4], refs[5:8], refs[8:11]
    outs, held = refs[11:15], refs[15]
    core = spot_ref[0]
    first = pl.ds(pl.multiple_of(core * HD, HD), HD)
    second = pl.ds(pl.multiple_of((1 - core) * HD, HD), HD)
    total = jnp.dot(rows[0][...], own[...], preferred_element_type=jnp.float32)
    for row, left, right in zip(rows[1:], mine, theirs):
        total += jnp.dot(
            jnp.concatenate([row[:, first], row[:, second]], axis=1),
            jnp.concatenate([left[...], right[...]], axis=0),
            preferred_element_type=jnp.float32,
        )
    held[...] = total
    n_rows = outs[0].shape[0]
    for far, out_ref in zip((0, *ORDER), outs):
        start = (spot_ref[1] + far) % SIDE * n_rows
        at = pl.ds(pl.multiple_of(start, n_rows), n_rows)
        out_ref[...] = held[at, :].astype(jnp.bfloat16)


def project(spot, rows, own, mine, theirs):
    n = len(mine)
    n_rows, depth = rows[0].shape
    width, tile = own.shape[1], 896
    return pl.pallas_call(
        project_kernel,
        grid=(width // tile,),
        in_specs=[pl.BlockSpec(memory_space=pltpu.SMEM)]
        + [pl.BlockSpec((n_rows, depth), lambda i: (0, 0))] * (1 + n)
        + [pl.BlockSpec((depth, tile), lambda i: (0, i))]
        + [pl.BlockSpec((HD, tile), lambda i: (0, i))] * n
        + [pl.BlockSpec((HD, tile), lambda i, k=k: (k, i)) for k in (0, 1, 0)],
        out_specs=[pl.BlockSpec((n_rows // SIDE, tile), lambda i: (0, i))] * SIDE,
        out_shape=[jax.ShapeDtypeStruct((n_rows // SIDE, width), jnp.bfloat16)] * SIDE,
        scratch_shapes=[pltpu.VMEM((n_rows, tile), jnp.float32)],
        compiler_params=pltpu.CompilerParams(vmem_limit_bytes=60 * 1024 * 1024),
        cost_estimate=pl.CostEstimate(
            flops=6 * n * n_rows * depth * width,
            bytes_accessed=2 * n * (n_rows * depth + depth * width) + 2 * n_rows * width,
            transcendentals=0,
        ),
        name="project",
    )(spot, *rows, own, *mine, theirs[0], theirs[0], theirs[1])


def chip_perm(far):
    return [
        (z * CORES + c, (z + far) * CORES + c) for z in range(SIDE - far) for c in range(CORES)
    ]


def ring_x(array, far):
    perm = [(x * SIDE + y, (x + far) % SIDE * SIDE + y) for x in range(SIDE) for y in range(SIDE)]
    return lax.ppermute(array, "exp", perm)


def ring_y(array, far):
    perm = [(x * SIDE + y, x * SIDE + (y + far) % SIDE) for x in range(SIDE) for y in range(SIDE)]
    return lax.ppermute(array, "exp", perm)


def swap_cores(array):
    perm = [(i, i ^ 1) for i in range(SIDE * CORES)]
    return lax.ppermute(array, "seq", perm)


def after(array, *earlier):
    return lax.optimization_barrier((array, *earlier))[0]


def attend(queries, keys, values, gates, share, send_share, early):
    me = lax.axis_index("seq")
    chip, core = me // CORES, me % CORES
    wanted = gates[me, 1:]
    codes = jnp.where(
        wanted == me, 0, jnp.where(wanted % CORES == core, chip - wanted // CORES, SIDE)
    )
    codes = jnp.append(codes, lax.axis_index("exp") // SIDE).astype(jnp.int32)
    partner_far = jnp.clip(chip - gates[me ^ 1, 1:] // CORES, 0, SIDE - 1).astype(jnp.int32)
    kv = jnp.stack([keys, values])
    near = [lax.ppermute(kv, "seq", chip_perm(far)) for far in range(1, SIDE)]
    mine = [send_share(share, 1), send_share(share, 3)]
    mine.append(send_share(after(share, *mine), 2))
    state = attend_own(queries, kv)
    joined = jnp.concatenate(mine[:2])
    near, mine, joined, state, early = lax.optimization_barrier(
        (near, mine, joined, state, early)
    )
    heads = range(queries.shape[1] // HD)
    asked = [choose(partner_far, [kv, *near], head) for head in heads]
    swapped = [swap_cores(block) for block in asked]
    theirs = [swap_cores(after(part, asked[-1])) for part in (joined, mine[2])]
    attn = None
    for head in heads:
        attn = attend_far(codes, queries, state, near, swapped[head], head, attn)
    return attn, mine, theirs, early


def projected(queries, keys, values, gates, o_proj, early):
    core = lax.axis_index("seq") % CORES
    share = lax.dynamic_slice(o_proj, (core * HD, 0), (HD, o_proj.shape[1]))
    pieces, mine, theirs, early = attend(queries, keys, values, gates, share, ring_x, early)
    rows = [pieces[0]] + [ring_x(piece, far) for piece, far in zip(pieces[1:], ORDER)]
    spot = jnp.stack([core, lax.axis_index("exp") % SIDE]).astype(jnp.int32)
    sums = project(spot, rows, o_proj, mine, theirs)
    total = sums[0].astype(jnp.float32)
    for piece, far in zip(sums[1:], ORDER):
        total = total + ring_y(piece, far).astype(jnp.float32)
    return total.astype(jnp.bfloat16), early


def expert_kernel(n_ff, rows_ref, gate_ref, up_ref, down_ref, out_ref, hidden_ref):
    step = pl.program_id(0)
    ff_tile = gate_ref.shape[2]

    @pl.when(step < n_ff)
    def _():
        rows = rows_ref[...]
        gate = jnp.dot(rows, gate_ref[0], preferred_element_type=jnp.float32)
        up = jnp.dot(rows, up_ref[0], preferred_element_type=jnp.float32)
        hidden = gate / (1.0 + jnp.exp(-gate)) * up
        cols = pl.ds(pl.multiple_of(step * ff_tile, ff_tile), ff_tile)
        hidden_ref[:, cols] = hidden.astype(jnp.bfloat16)

    @pl.when(step >= n_ff)
    def _():
        out_ref[...] = jnp.dot(
            hidden_ref[...], down_ref[0], preferred_element_type=jnp.float32
        ).astype(jnp.bfloat16)


def expert_rows(rows, w_gate, w_up, w_down):
    n_rows, width = rows.shape
    ff = w_gate.shape[2]
    ff_tile, out_tile = 256, 512
    n_ff, n_out = ff // ff_tile, width // out_tile

    def ff_at(i):
        return (0, 0, jnp.minimum(i, n_ff - 1))

    def out_at(i):
        return jnp.maximum(i - n_ff, 0)

    return pl.pallas_call(
        lambda *refs: expert_kernel(n_ff, *refs),
        grid=(n_ff + n_out,),
        in_specs=[
            pl.BlockSpec(memory_space=pltpu.VMEM),
            pl.BlockSpec((1, width, ff_tile), ff_at),
            pl.BlockSpec((1, width, ff_tile), ff_at),
            pl.BlockSpec((1, ff, out_tile), lambda i: (0, 0, out_at(i))),
        ],
        out_specs=pl.BlockSpec((n_rows, out_tile), lambda i: (0, out_at(i))),
        out_shape=pltpu.HBM((n_rows, width), jnp.bfloat16),
        scratch_shapes=[pltpu.VMEM((n_rows, ff), jnp.bfloat16)],
        compiler_params=pltpu.CompilerParams(vmem_limit_bytes=32 * 1024 * 1024),
        cost_estimate=pl.CostEstimate(
            flops=6 * n_rows * width * ff,
            bytes_accessed=2 * (2 * n_rows * width + 3 * width * ff),
            transcendentals=n_rows * ff,
        ),
        name="experts",
    )(rows, w_gate, w_up, w_down)


def slot_tables(routes, route_weights, n_experts, cap):
    n_tok, n_slots = routes.shape[0], n_experts * cap
    hit = jnp.zeros((n_tok, n_experts), jnp.bool_)
    weight = jnp.zeros((n_tok, n_experts), jnp.float32)
    expert_ids = lax.broadcasted_iota(jnp.int32, (n_tok, n_experts), 1)
    for k in range(routes.shape[1]):
        match = routes[:, k : k + 1] == expert_ids
        hit = jnp.logical_or(hit, match)
        weight = weight + jnp.where(match, route_weights[:, k : k + 1], 0.0)
    square = (n_tok, n_tok)
    ahead = lax.broadcasted_iota(jnp.int32, square, 0) > lax.broadcasted_iota(jnp.int32, square, 1)
    rank = jnp.dot(
        ahead.astype(jnp.bfloat16), hit.astype(jnp.bfloat16), preferred_element_type=jnp.float32
    )
    place = jnp.where(hit, rank, float(2 * n_tok)).astype(jnp.bfloat16)
    high = weight.astype(jnp.bfloat16)
    low = (weight - high.astype(jnp.float32)).astype(jnp.bfloat16)
    spread = lax.broadcasted_iota(jnp.int32, (n_experts, n_slots), 0) == (
        lax.broadcasted_iota(jnp.int32, (n_experts, n_slots), 1) // cap
    )
    wide = jnp.dot(
        jnp.concatenate([place, high, low], axis=0),
        spread.astype(jnp.bfloat16),
        preferred_element_type=jnp.float32,
    )
    slot_ids = lax.broadcasted_iota(jnp.int32, (n_tok, n_slots), 1) % cap
    taken = wide[:n_tok] == slot_ids.astype(jnp.float32)
    pick = taken.astype(jnp.bfloat16)
    mix = jnp.where(jnp.concatenate([taken, taken], axis=0), wide[n_tok:], 0.0)
    return pick.T, mix.astype(jnp.bfloat16)


def combine_kernel(mix_ref, rows_ref, out_ref):
    n_tok, tile = out_ref.shape
    cols = pl.ds(pl.multiple_of(pl.program_id(0) * tile, tile), tile)
    halves = jnp.dot(mix_ref[...], rows_ref[:, cols], preferred_element_type=jnp.float32)
    out_ref[...] = (halves[:n_tok] + halves[n_tok:]).astype(jnp.bfloat16)


def combine(mix, rows):
    n_rows, width = rows.shape
    n_tok, tile = mix.shape[0] // 2, 896
    return pl.pallas_call(
        combine_kernel,
        grid=(width // tile,),
        in_specs=[pl.BlockSpec(memory_space=pltpu.VMEM)] * 2,
        out_specs=pl.BlockSpec((n_tok, tile), lambda i: (0, i)),
        out_shape=jax.ShapeDtypeStruct((n_tok, width), jnp.bfloat16),
        compiler_params=pltpu.CompilerParams(vmem_limit_bytes=24 * 1024 * 1024),
        cost_estimate=pl.CostEstimate(
            flops=4 * n_tok * n_rows * width, bytes_accessed=2 * n_rows * width, transcendentals=0
        ),
        name="combine",
    )(mix, rows)


def per_device(
    queries,
    keys,
    values,
    gates,
    o_proj,
    residual,
    norm_gain,
    routes,
    route_weights,
    w_gate,
    w_up,
    w_down,
):
    tok_moe, width = residual.shape
    n_experts = w_gate.shape[0] * lax.axis_size("seq") * lax.axis_size("exp")
    cap = 2 * tok_moe * ROUTE_K // n_experts
    tables = slot_tables(routes, route_weights, n_experts, cap)
    summed, (place, mix) = projected(queries, keys, values, gates, o_proj, tables)
    residual_sum = residual.astype(jnp.float32) + summed.astype(jnp.float32)
    norm_scale = lax.rsqrt(jnp.mean(residual_sum * residual_sum, axis=-1, keepdims=True) + 1e-06)
    moe_in = (residual_sum * norm_scale * norm_gain).astype(jnp.bfloat16)
    senders = jnp.dot(place, moe_in, preferred_element_type=jnp.float32).astype(jnp.bfloat16)
    received = lax.all_to_all(
        senders.reshape(n_experts, cap, width),
        ("seq", "exp"),
        split_axis=0,
        concat_axis=0,
        tiled=True,
    )
    produced = expert_rows(received.reshape(n_experts * cap, width), w_gate, w_up, w_down)
    returned = lax.all_to_all(
        produced.reshape(n_experts, cap, width),
        ("seq", "exp"),
        split_axis=0,
        concat_axis=0,
        tiled=True,
    )
    moe_out = combine(mix, returned.reshape(n_experts * cap, width))
    return (summed, moe_out)


def solution(mesh):
    in_specs = (
        P("seq", "exp"),
        P("seq", "exp"),
        P("seq", "exp"),
        P(),
        P("exp", None),
        P(("seq", "exp"), None),
        P(),
        P(("seq", "exp"), None),
        P(("seq", "exp"), None),
        P(("seq", "exp"), None, None),
        P(("seq", "exp"), None, None),
        P(("seq", "exp"), None, None),
    )
    out_specs = (P(("seq", "exp"), None), P(("seq", "exp"), None))
    return jax.shard_map(
        per_device, mesh=mesh, in_specs=in_specs, out_specs=out_specs, check_vma=False
    )
```

```python
import math

import jax
import jax.numpy as jnp
from jax import lax
from jax.experimental import pallas as pl
from jax.experimental.pallas import tpu as pltpu
from jax.sharding import PartitionSpec as P

HD = 128
BLOCK = 1024
ROUTE_K = 8


NEG_FILL = -1e30
SCALE = math.log2(math.e) / math.sqrt(HD)
Q_TILE = 128
CORES = 2
SIDE = 4
ORDER = (1, 3, 2)


def dot_t(a, b):
    return lax.dot_general(a, b, (((1,), (1,)), ((), ())), preferred_element_type=jnp.float32)


def mix_values(weights, values):
    wide = jnp.concatenate([values, jnp.ones_like(values)], axis=1)
    both = jnp.dot(weights.astype(jnp.bfloat16), wide, preferred_element_type=jnp.float32)
    return both[:, :HD], both[:, HD:]


def own_kernel(q_ref, kv_ref, top_ref, sum_ref, acc_ref):
    for i in range(q_ref.shape[0] // Q_TILE):
        at = pl.ds(i * Q_TILE, Q_TILE)
        seen = pl.ds(0, (i + 1) * Q_TILE)
        scores = dot_t(q_ref[at, :], kv_ref[0, seen, :])
        query_pos = lax.broadcasted_iota(jnp.int32, scores.shape, 0) + i * Q_TILE
        key_pos = lax.broadcasted_iota(jnp.int32, scores.shape, 1)
        scores = jnp.where(key_pos <= query_pos, scores, NEG_FILL)
        top = jnp.max(scores, axis=1, keepdims=True)
        weights = jnp.exp2((scores - top) * SCALE)
        acc, amount = mix_values(weights, kv_ref[1, seen, :])
        top_ref[at, :] = jnp.broadcast_to(top, (Q_TILE, HD))
        sum_ref[at, :] = amount
        acc_ref[at, :] = acc


def attend_own(queries, kv):
    n, width = queries.shape
    spec = pl.BlockSpec((n, HD), lambda h: (0, h))
    return pl.pallas_call(
        own_kernel,
        grid=(width // HD,),
        in_specs=[spec, pl.BlockSpec((2, n, HD), lambda h: (0, 0, h))],
        out_specs=[spec] * 3,
        out_shape=[jax.ShapeDtypeStruct((n, width), jnp.float32)] * 3,
        compiler_params=pltpu.CompilerParams(vmem_limit_bytes=60 * 1024 * 1024),
        cost_estimate=pl.CostEstimate(
            flops=8 * n * n * width, bytes_accessed=18 * n * width, transcendentals=n * n
        ),
        name="attend_own",
    )(queries, kv)


def far_kernel(code_ref, q_ref, top_ref, sum_ref, acc_ref, *refs):
    near, swapped, outs = refs[: SIDE - 1], refs[SIDE - 1], refs[SIDE : 2 * SIDE]
    held, tops, sums, accs = refs[-4:]
    tops[...] = top_ref[...]
    sums[...] = sum_ref[...]
    accs[...] = acc_ref[...]
    for j in range(swapped.shape[0]):
        code = code_ref[j]
        for s in range(len(near)):

            @pl.when(code == s + 1)
            def _(s=s):
                held[...] = near[s][...]

        @pl.when(code == len(near) + 1)
        def _(j=j):
            held[...] = swapped[j]

        @pl.when(code > 0)
        def _():
            for i in range(q_ref.shape[0] // Q_TILE):
                at = pl.ds(i * Q_TILE, Q_TILE)
                scores = dot_t(q_ref[at, :], held[0])
                old = tops[at, :]
                top = jnp.maximum(old, jnp.max(scores, axis=1, keepdims=True))
                weights = jnp.exp2((scores - top[:, :1]) * SCALE)
                fade = jnp.exp2((old - top) * SCALE)
                acc, amount = mix_values(weights, held[1])
                tops[at, :] = top
                sums[at, :] = sums[at, :] * fade + amount
                accs[at, :] = accs[at, :] * fade + acc

    n_rows = outs[0].shape[0]
    for far, out_ref in zip((0, *ORDER), outs):
        start = (code_ref[swapped.shape[0]] + far) % SIDE * n_rows
        at = pl.ds(pl.multiple_of(start, n_rows), n_rows)
        out_ref[...] = (accs[at, :] / sums[at, :]).astype(jnp.bfloat16)


def attend_far(codes, queries, state, near, swapped, head, before):
    n, width = queries.shape
    spec = pl.BlockSpec((n, HD), lambda i: (0, head))
    extra = [] if before is None else before
    return pl.pallas_call(
        lambda *refs: far_kernel(*refs[len(extra) :]),
        grid=(1,),
        in_specs=[pl.BlockSpec(memory_space=pl.ANY)] * len(extra)
        + [pl.BlockSpec(memory_space=pltpu.SMEM)]
        + [spec] * 4
        + [pl.BlockSpec((2, n, HD), lambda i: (0, 0, head))] * len(near)
        + [pl.BlockSpec(swapped.shape, lambda i: (0, 0, 0, 0))],
        out_specs=[pl.BlockSpec((n // SIDE, HD), lambda i: (0, head))] * SIDE,
        out_shape=[jax.ShapeDtypeStruct((n // SIDE, width), jnp.bfloat16)] * SIDE,
        input_output_aliases={i: i for i in range(len(extra))},
        scratch_shapes=[pltpu.VMEM((2, n, HD), jnp.bfloat16)]
        + [pltpu.VMEM((n, HD), jnp.float32)] * 3,
        compiler_params=pltpu.CompilerParams(vmem_limit_bytes=32 * 1024 * 1024),
        cost_estimate=pl.CostEstimate(
            flops=48 * n * n * HD, bytes_accessed=24 * n * HD, transcendentals=2 * n * n
        ),
        name="attend_far",
    )(*extra, codes, queries, *state, *near, swapped)


def choose_kernel(far_ref, *refs):
    blocks, out_ref = refs[:-1], refs[-1]
    for j in range(out_ref.shape[0]):
        for far, block in enumerate(blocks):

            @pl.when(far_ref[j] == far)
            def _(j=j, block=block):
                out_ref[j] = block[...]


def choose(fars, blocks, head):
    n = blocks[0].shape[1]
    count = fars.shape[0]
    return pl.pallas_call(
        choose_kernel,
        grid=(2, 2),
        in_specs=[pl.BlockSpec(memory_space=pltpu.SMEM)]
        + [pl.BlockSpec((1, n // 2, HD), lambda i, k: (i, k, head))] * len(blocks),
        out_specs=pl.BlockSpec((count, 1, n // 2, HD), lambda i, k: (0, i, k, 0)),
        out_shape=jax.ShapeDtypeStruct((count, 2, n, HD), jnp.bfloat16),
        compiler_params=pltpu.CompilerParams(vmem_limit_bytes=16 * 1024 * 1024),
        cost_estimate=pl.CostEstimate(flops=0, bytes_accessed=24 * n * HD, transcendentals=0),
        name="choose",
    )(fars, *blocks)


def project_kernel(spot_ref, *refs):
    rows, own, mine, theirs = refs[:4], refs[4], refs[5:8], refs[8:11]
    outs, held = refs[11:15], refs[15]
    core = spot_ref[0]
    first = pl.ds(pl.multiple_of(core * HD, HD), HD)
    second = pl.ds(pl.multiple_of((1 - core) * HD, HD), HD)
    total = jnp.dot(rows[0][...], own[...], preferred_element_type=jnp.float32)
    for row, left, right in zip(rows[1:], mine, theirs):
        total += jnp.dot(
            jnp.concatenate([row[:, first], row[:, second]], axis=1),
            jnp.concatenate([left[...], right[...]], axis=0),
            preferred_element_type=jnp.float32,
        )
    held[...] = total
    n_rows = outs[0].shape[0]
    for far, out_ref in zip((0, *ORDER), outs):
        start = (spot_ref[1] + far) % SIDE * n_rows
        at = pl.ds(pl.multiple_of(start, n_rows), n_rows)
        out_ref[...] = held[at, :].astype(jnp.bfloat16)


def project(spot, rows, own, mine, theirs):
    n = len(mine)
    n_rows, depth = rows[0].shape
    width, tile = own.shape[1], 896
    return pl.pallas_call(
        project_kernel,
        grid=(width // tile,),
        in_specs=[pl.BlockSpec(memory_space=pltpu.SMEM)]
        + [pl.BlockSpec((n_rows, depth), lambda i: (0, 0))] * (1 + n)
        + [pl.BlockSpec((depth, tile), lambda i: (0, i))]
        + [pl.BlockSpec((HD, tile), lambda i: (0, i))] * n
        + [pl.BlockSpec((HD, tile), lambda i, k=k: (k, i)) for k in (0, 1, 0)],
        out_specs=[pl.BlockSpec((n_rows // SIDE, tile), lambda i: (0, i))] * SIDE,
        out_shape=[jax.ShapeDtypeStruct((n_rows // SIDE, width), jnp.bfloat16)] * SIDE,
        scratch_shapes=[pltpu.VMEM((n_rows, tile), jnp.float32)],
        compiler_params=pltpu.CompilerParams(vmem_limit_bytes=44 * 1024 * 1024),
        cost_estimate=pl.CostEstimate(
            flops=6 * n * n_rows * depth * width,
            bytes_accessed=2 * n * (n_rows * depth + depth * width) + 2 * n_rows * width,
            transcendentals=0,
        ),
        name="project",
    )(spot, *rows, own, *mine, theirs[0], theirs[0], theirs[1])


def chip_perm(far):
    return [
        (z * CORES + c, (z + far) * CORES + c) for z in range(SIDE - far) for c in range(CORES)
    ]


def ring_x(array, far):
    perm = [(x * SIDE + y, (x + far) % SIDE * SIDE + y) for x in range(SIDE) for y in range(SIDE)]
    return lax.ppermute(array, "exp", perm)


def ring_y(array, far):
    perm = [(x * SIDE + y, x * SIDE + (y + far) % SIDE) for x in range(SIDE) for y in range(SIDE)]
    return lax.ppermute(array, "exp", perm)


def swap_cores(array):
    perm = [(i, i ^ 1) for i in range(SIDE * CORES)]
    return lax.ppermute(array, "seq", perm)


def after(array, *earlier):
    return lax.optimization_barrier((array, *earlier))[0]


def attend(queries, keys, values, gates, share, send_share, early):
    me = lax.axis_index("seq")
    chip, core = me // CORES, me % CORES
    wanted = gates[me, 1:]
    codes = jnp.where(
        wanted == me, 0, jnp.where(wanted % CORES == core, chip - wanted // CORES, SIDE)
    )
    codes = jnp.append(codes, lax.axis_index("exp") // SIDE).astype(jnp.int32)
    partner_far = jnp.clip(chip - gates[me ^ 1, 1:] // CORES, 0, SIDE - 1).astype(jnp.int32)
    kv = jnp.stack([keys, values])
    near = [lax.ppermute(kv, "seq", chip_perm(far)) for far in range(1, SIDE)]
    mine = [send_share(share, 1), send_share(share, 3)]
    mine.append(send_share(after(share, *mine), 2))
    state = attend_own(queries, kv)
    joined = jnp.concatenate(mine[:2])
    near, mine, joined, state, early, codes, partner_far = lax.optimization_barrier(
        (near, mine, joined, state, early, codes, partner_far)
    )
    heads = range(queries.shape[1] // HD)
    asked = [choose(partner_far, [kv, *near], head) for head in heads]
    swapped = [swap_cores(block) for block in asked]
    theirs = [swap_cores(after(part, asked[-1])) for part in (joined, mine[2])]
    attn = None
    for head in heads:
        attn = attend_far(codes, queries, state, near, swapped[head], head, attn)
    return attn, mine, theirs, early


def projected(queries, keys, values, gates, o_proj, early):
    core = lax.axis_index("seq") % CORES
    share = lax.dynamic_slice(o_proj, (core * HD, 0), (HD, o_proj.shape[1]))
    pieces, mine, theirs, early = attend(queries, keys, values, gates, share, ring_x, early)
    rows = [pieces[0]] + [ring_x(piece, far) for piece, far in zip(pieces[1:], ORDER)]
    spot = jnp.stack([core, lax.axis_index("exp") % SIDE]).astype(jnp.int32)
    sums = project(spot, rows, o_proj, mine, theirs)
    total = sums[0].astype(jnp.float32)
    for piece, far in zip(sums[1:], ORDER):
        total = total + ring_y(piece, far).astype(jnp.float32)
    return total.astype(jnp.bfloat16), early


def expert_kernel(n_ff, rows_ref, gate_ref, up_ref, down_ref, out_ref, hidden_ref):
    step = pl.program_id(0)
    ff_tile = gate_ref.shape[2]

    @pl.when(step < n_ff)
    def _():
        rows = rows_ref[...]
        gate = jnp.dot(rows, gate_ref[0], preferred_element_type=jnp.float32)
        up = jnp.dot(rows, up_ref[0], preferred_element_type=jnp.float32)
        hidden = gate / (1.0 + jnp.exp(-gate)) * up
        cols = pl.ds(pl.multiple_of(step * ff_tile, ff_tile), ff_tile)
        hidden_ref[:, cols] = hidden.astype(jnp.bfloat16)

    @pl.when(step >= n_ff)
    def _():
        out_ref[...] = jnp.dot(
            hidden_ref[...], down_ref[0], preferred_element_type=jnp.float32
        ).astype(jnp.bfloat16)


def expert_rows(rows, w_gate, w_up, w_down):
    n_rows, width = rows.shape
    ff = w_gate.shape[2]
    ff_tile, out_tile = 256, 512
    n_ff, n_out = ff // ff_tile, width // out_tile

    def ff_at(i):
        return (0, 0, jnp.minimum(i, n_ff - 1))

    def out_at(i):
        return jnp.maximum(i - n_ff, 0)

    return pl.pallas_call(
        lambda *refs: expert_kernel(n_ff, *refs),
        grid=(n_ff + n_out,),
        in_specs=[
            pl.BlockSpec(memory_space=pltpu.VMEM),
            pl.BlockSpec((1, width, ff_tile), ff_at),
            pl.BlockSpec((1, width, ff_tile), ff_at),
            pl.BlockSpec((1, ff, out_tile), lambda i: (0, 0, out_at(i))),
        ],
        out_specs=pl.BlockSpec((n_rows, out_tile), lambda i: (0, out_at(i))),
        out_shape=pltpu.HBM((n_rows, width), jnp.bfloat16),
        scratch_shapes=[pltpu.VMEM((n_rows, ff), jnp.bfloat16)],
        compiler_params=pltpu.CompilerParams(vmem_limit_bytes=32 * 1024 * 1024),
        cost_estimate=pl.CostEstimate(
            flops=6 * n_rows * width * ff,
            bytes_accessed=2 * (2 * n_rows * width + 3 * width * ff),
            transcendentals=n_rows * ff,
        ),
        name="experts",
    )(rows, w_gate, w_up, w_down)


def slot_tables(routes, route_weights, n_experts, cap):
    n_tok, n_slots = routes.shape[0], n_experts * cap
    hit = jnp.zeros((n_tok, n_experts), jnp.bool_)
    weight = jnp.zeros((n_tok, n_experts), jnp.float32)
    expert_ids = lax.broadcasted_iota(jnp.int32, (n_tok, n_experts), 1)
    for k in range(routes.shape[1]):
        match = routes[:, k : k + 1] == expert_ids
        hit = jnp.logical_or(hit, match)
        weight = weight + jnp.where(match, route_weights[:, k : k + 1], 0.0)
    square = (n_tok, n_tok)
    ahead = lax.broadcasted_iota(jnp.int32, square, 0) > lax.broadcasted_iota(jnp.int32, square, 1)
    rank = jnp.dot(
        ahead.astype(jnp.bfloat16), hit.astype(jnp.bfloat16), preferred_element_type=jnp.float32
    )
    place = jnp.where(hit, rank, float(2 * n_tok)).astype(jnp.bfloat16)
    high = weight.astype(jnp.bfloat16)
    low = (weight - high.astype(jnp.float32)).astype(jnp.bfloat16)
    spread = lax.broadcasted_iota(jnp.int32, (n_experts, n_slots), 0) == (
        lax.broadcasted_iota(jnp.int32, (n_experts, n_slots), 1) // cap
    )
    wide = jnp.dot(
        jnp.concatenate([place, high, low], axis=0),
        spread.astype(jnp.bfloat16),
        preferred_element_type=jnp.float32,
    )
    slot_ids = lax.broadcasted_iota(jnp.int32, (n_tok, n_slots), 1) % cap
    taken = wide[:n_tok] == slot_ids.astype(jnp.float32)
    pick = taken.astype(jnp.bfloat16)
    mix = jnp.where(jnp.concatenate([taken, taken], axis=0), wide[n_tok:], 0.0)
    return pick.T, mix.astype(jnp.bfloat16)


def combine_kernel(mix_ref, rows_ref, out_ref):
    n_tok, tile = out_ref.shape
    cols = pl.ds(pl.multiple_of(pl.program_id(0) * tile, tile), tile)
    halves = jnp.dot(mix_ref[...], rows_ref[:, cols], preferred_element_type=jnp.float32)
    out_ref[...] = (halves[:n_tok] + halves[n_tok:]).astype(jnp.bfloat16)


def combine(mix, rows):
    n_rows, width = rows.shape
    n_tok, tile = mix.shape[0] // 2, 896
    return pl.pallas_call(
        combine_kernel,
        grid=(width // tile,),
        in_specs=[pl.BlockSpec(memory_space=pltpu.VMEM)] * 2,
        out_specs=pl.BlockSpec((n_tok, tile), lambda i: (0, i)),
        out_shape=jax.ShapeDtypeStruct((n_tok, width), jnp.bfloat16),
        compiler_params=pltpu.CompilerParams(vmem_limit_bytes=24 * 1024 * 1024),
        cost_estimate=pl.CostEstimate(
            flops=4 * n_tok * n_rows * width, bytes_accessed=2 * n_rows * width, transcendentals=0
        ),
        name="combine",
    )(mix, rows)


def per_device(
    queries,
    keys,
    values,
    gates,
    o_proj,
    residual,
    norm_gain,
    routes,
    route_weights,
    w_gate,
    w_up,
    w_down,
):
    tok_moe, width = residual.shape
    n_experts = w_gate.shape[0] * lax.axis_size("seq") * lax.axis_size("exp")
    cap = 2 * tok_moe * ROUTE_K // n_experts
    tables = slot_tables(routes, route_weights, n_experts, cap)
    summed, (place, mix) = projected(queries, keys, values, gates, o_proj, tables)
    residual_sum = residual.astype(jnp.float32) + summed.astype(jnp.float32)
    norm_scale = lax.rsqrt(jnp.mean(residual_sum * residual_sum, axis=-1, keepdims=True) + 1e-06)
    moe_in = (residual_sum * norm_scale * norm_gain).astype(jnp.bfloat16)
    senders = jnp.dot(place, moe_in, preferred_element_type=jnp.float32).astype(jnp.bfloat16)
    received = lax.all_to_all(
        senders.reshape(n_experts, cap, width),
        ("seq", "exp"),
        split_axis=0,
        concat_axis=0,
        tiled=True,
    )
    produced = expert_rows(received.reshape(n_experts * cap, width), w_gate, w_up, w_down)
    returned = lax.all_to_all(
        produced.reshape(n_experts, cap, width),
        ("seq", "exp"),
        split_axis=0,
        concat_axis=0,
        tiled=True,
    )
    moe_out = combine(mix, returned.reshape(n_experts * cap, width))
    return (summed, moe_out)


def solution(mesh):
    in_specs = (
        P("seq", "exp"),
        P("seq", "exp"),
        P("seq", "exp"),
        P(),
        P("exp", None),
        P(("seq", "exp"), None),
        P(),
        P(("seq", "exp"), None),
        P(("seq", "exp"), None),
        P(("seq", "exp"), None, None),
        P(("seq", "exp"), None, None),
        P(("seq", "exp"), None, None),
    )
    out_specs = (P(("seq", "exp"), None), P(("seq", "exp"), None))
    return jax.shard_map(
        per_device, mesh=mesh, in_specs=in_specs, out_specs=out_specs, check_vma=False
    )
```

```python
import math

import jax
import jax.numpy as jnp
from jax import lax
from jax.experimental import pallas as pl
from jax.experimental.pallas import tpu as pltpu
from jax.sharding import PartitionSpec as P

HD = 128
BLOCK = 1024
ROUTE_K = 8


NEG_FILL = -1e30
SCALE = math.log2(math.e) / math.sqrt(HD)
Q_TILE = 128
CORES = 2
SIDE = 4
ORDER = (1, 3, 2)


def dot_t(a, b):
    return lax.dot_general(a, b, (((1,), (1,)), ((), ())), preferred_element_type=jnp.float32)


def mix_values(weights, values):
    wide = jnp.concatenate([values, jnp.ones_like(values)], axis=1)
    both = jnp.dot(weights.astype(jnp.bfloat16), wide, preferred_element_type=jnp.float32)
    return both[:, :HD], both[:, HD:]


def own_kernel(q_ref, kv_ref, top_ref, sum_ref, acc_ref):
    for i in range(q_ref.shape[0] // Q_TILE):
        at = pl.ds(i * Q_TILE, Q_TILE)
        seen = pl.ds(0, (i + 1) * Q_TILE)
        scores = dot_t(q_ref[at, :], kv_ref[0, seen, :])
        query_pos = lax.broadcasted_iota(jnp.int32, scores.shape, 0) + i * Q_TILE
        key_pos = lax.broadcasted_iota(jnp.int32, scores.shape, 1)
        scores = jnp.where(key_pos <= query_pos, scores, NEG_FILL)
        top = jnp.max(scores, axis=1, keepdims=True)
        weights = jnp.exp2((scores - top) * SCALE)
        acc, amount = mix_values(weights, kv_ref[1, seen, :])
        top_ref[at, :] = jnp.broadcast_to(top, (Q_TILE, HD))
        sum_ref[at, :] = amount
        acc_ref[at, :] = acc


def attend_own(queries, kv):
    n, width = queries.shape
    spec = pl.BlockSpec((n, HD), lambda h: (0, h))
    return pl.pallas_call(
        own_kernel,
        grid=(width // HD,),
        in_specs=[spec, pl.BlockSpec((2, n, HD), lambda h: (0, 0, h))],
        out_specs=[spec] * 3,
        out_shape=[jax.ShapeDtypeStruct((n, width), jnp.float32)] * 3,
        compiler_params=pltpu.CompilerParams(vmem_limit_bytes=60 * 1024 * 1024),
        cost_estimate=pl.CostEstimate(
            flops=8 * n * n * width, bytes_accessed=18 * n * width, transcendentals=n * n
        ),
        name="attend_own",
    )(queries, kv)


def far_kernel(code_ref, q_ref, top_ref, sum_ref, acc_ref, *refs):
    near, swapped, outs = refs[: SIDE - 1], refs[SIDE - 1], refs[SIDE : 2 * SIDE]
    held, tops, sums, accs = refs[-4:]
    tops[...] = top_ref[...]
    sums[...] = sum_ref[...]
    accs[...] = acc_ref[...]
    for j in range(swapped.shape[0]):
        code = code_ref[j]
        for s in range(len(near)):

            @pl.when(code == s + 1)
            def _(s=s):
                held[...] = near[s][...]

        @pl.when(code == len(near) + 1)
        def _(j=j):
            held[...] = swapped[j]

        @pl.when(code > 0)
        def _():
            for i in range(q_ref.shape[0] // Q_TILE):
                at = pl.ds(i * Q_TILE, Q_TILE)
                scores = dot_t(q_ref[at, :], held[0])
                old = tops[at, :]
                top = jnp.maximum(old, jnp.max(scores, axis=1, keepdims=True))
                weights = jnp.exp2((scores - top[:, :1]) * SCALE)
                fade = jnp.exp2((old - top) * SCALE)
                acc, amount = mix_values(weights, held[1])
                tops[at, :] = top
                sums[at, :] = sums[at, :] * fade + amount
                accs[at, :] = accs[at, :] * fade + acc

    n_rows = outs[0].shape[0]
    for far, out_ref in zip((0, *ORDER), outs):
        start = (code_ref[swapped.shape[0]] + far) % SIDE * n_rows
        at = pl.ds(pl.multiple_of(start, n_rows), n_rows)
        out_ref[...] = (accs[at, :] / sums[at, :]).astype(jnp.bfloat16)


def attend_far(codes, queries, state, near, swapped, head, before):
    n, width = queries.shape
    spec = pl.BlockSpec((n, HD), lambda i: (0, head))
    extra = [] if before is None else before
    return pl.pallas_call(
        lambda *refs: far_kernel(*refs[len(extra) :]),
        grid=(1,),
        in_specs=[pl.BlockSpec(memory_space=pl.ANY)] * len(extra)
        + [pl.BlockSpec(memory_space=pltpu.SMEM)]
        + [spec] * 4
        + [pl.BlockSpec((2, n, HD), lambda i: (0, 0, head))] * len(near)
        + [pl.BlockSpec(swapped.shape, lambda i: (0, 0, 0, 0))],
        out_specs=[pl.BlockSpec((n // SIDE, HD), lambda i: (0, head))] * SIDE,
        out_shape=[jax.ShapeDtypeStruct((n // SIDE, width), jnp.bfloat16)] * SIDE,
        input_output_aliases={i: i for i in range(len(extra))},
        scratch_shapes=[pltpu.VMEM((2, n, HD), jnp.bfloat16)]
        + [pltpu.VMEM((n, HD), jnp.float32)] * 3,
        compiler_params=pltpu.CompilerParams(vmem_limit_bytes=32 * 1024 * 1024),
        cost_estimate=pl.CostEstimate(
            flops=48 * n * n * HD, bytes_accessed=24 * n * HD, transcendentals=2 * n * n
        ),
        name="attend_far",
    )(*extra, codes, queries, *state, *near, swapped)


def choose_kernel(far_ref, *refs):
    blocks, out_ref = refs[:-1], refs[-1]
    for j in range(out_ref.shape[0]):
        for far, block in enumerate(blocks):

            @pl.when(far_ref[j] == far)
            def _(j=j, block=block):
                out_ref[j] = block[...]


def choose(fars, blocks, head):
    n = blocks[0].shape[1]
    count = fars.shape[0]
    return pl.pallas_call(
        choose_kernel,
        grid=(2, 2),
        in_specs=[pl.BlockSpec(memory_space=pltpu.SMEM)]
        + [pl.BlockSpec((1, n // 2, HD), lambda i, k: (i, k, head))] * len(blocks),
        out_specs=pl.BlockSpec((count, 1, n // 2, HD), lambda i, k: (0, i, k, 0)),
        out_shape=jax.ShapeDtypeStruct((count, 2, n, HD), jnp.bfloat16),
        compiler_params=pltpu.CompilerParams(vmem_limit_bytes=16 * 1024 * 1024),
        cost_estimate=pl.CostEstimate(flops=0, bytes_accessed=24 * n * HD, transcendentals=0),
        name="choose",
    )(fars, *blocks)


def project_kernel(spot_ref, *refs):
    rows, own, mine, theirs = refs[:4], refs[4], refs[5:8], refs[8:11]
    outs, held = refs[11:15], refs[15]
    core = spot_ref[0]
    first = pl.ds(pl.multiple_of(core * HD, HD), HD)
    second = pl.ds(pl.multiple_of((1 - core) * HD, HD), HD)
    total = jnp.dot(rows[0][...], own[...], preferred_element_type=jnp.float32)
    for row, left, right in zip(rows[1:], mine, theirs):
        total += jnp.dot(
            jnp.concatenate([row[:, first], row[:, second]], axis=1),
            jnp.concatenate([left[...], right[...]], axis=0),
            preferred_element_type=jnp.float32,
        )
    held[...] = total
    n_rows = outs[0].shape[0]
    for far, out_ref in zip((0, *ORDER), outs):
        start = (spot_ref[1] + far) % SIDE * n_rows
        at = pl.ds(pl.multiple_of(start, n_rows), n_rows)
        out_ref[...] = held[at, :].astype(jnp.bfloat16)


def project(spot, rows, own, mine, theirs):
    n = len(mine)
    n_rows, depth = rows[0].shape
    width, tile = own.shape[1], 896
    return pl.pallas_call(
        project_kernel,
        grid=(width // tile,),
        in_specs=[pl.BlockSpec(memory_space=pltpu.SMEM)]
        + [pl.BlockSpec((n_rows, depth), lambda i: (0, 0))] * (1 + n)
        + [pl.BlockSpec((depth, tile), lambda i: (0, i))]
        + [pl.BlockSpec((HD, tile), lambda i: (0, i))] * n
        + [pl.BlockSpec((HD, tile), lambda i, k=k: (k, i)) for k in (0, 1, 0)],
        out_specs=[pl.BlockSpec((n_rows // SIDE, tile), lambda i: (0, i))] * SIDE,
        out_shape=[jax.ShapeDtypeStruct((n_rows // SIDE, width), jnp.bfloat16)] * SIDE,
        scratch_shapes=[pltpu.VMEM((n_rows, tile), jnp.float32)],
        compiler_params=pltpu.CompilerParams(vmem_limit_bytes=44 * 1024 * 1024),
        cost_estimate=pl.CostEstimate(
            flops=6 * n * n_rows * depth * width,
            bytes_accessed=2 * n * (n_rows * depth + depth * width) + 2 * n_rows * width,
            transcendentals=0,
        ),
        name="project",
    )(spot, *rows, own, *mine, theirs[0], theirs[0], theirs[1])


def chip_perm(far):
    return [
        (z * CORES + c, (z + far) * CORES + c) for z in range(SIDE - far) for c in range(CORES)
    ]


def ring_x(array, far):
    perm = [(x * SIDE + y, (x + far) % SIDE * SIDE + y) for x in range(SIDE) for y in range(SIDE)]
    return lax.ppermute(array, "exp", perm)


def ring_y(array, far):
    perm = [(x * SIDE + y, x * SIDE + (y + far) % SIDE) for x in range(SIDE) for y in range(SIDE)]
    return lax.ppermute(array, "exp", perm)


def swap_cores(array):
    perm = [(i, i ^ 1) for i in range(SIDE * CORES)]
    return lax.ppermute(array, "seq", perm)


def after(array, *earlier):
    return lax.optimization_barrier((array, *earlier))[0]


def attend(queries, keys, values, gates, share_after, send_share, early):
    me = lax.axis_index("seq")
    chip, core = me // CORES, me % CORES
    wanted = gates[me, 1:]
    codes = jnp.where(
        wanted == me, 0, jnp.where(wanted % CORES == core, chip - wanted // CORES, SIDE)
    )
    codes = jnp.append(codes, lax.axis_index("exp") // SIDE).astype(jnp.int32)
    partner_far = jnp.clip(chip - gates[me ^ 1, 1:] // CORES, 0, SIDE - 1).astype(jnp.int32)
    kv = jnp.stack([keys, values])
    share = share_after(kv)
    near = [lax.ppermute(kv, "seq", chip_perm(far)) for far in range(1, SIDE)]
    mine = [send_share(share, 1), send_share(share, 3)]
    mine.append(send_share(after(share, *mine), 2))
    state = attend_own(queries, kv)
    joined = jnp.concatenate(mine[:2])
    near, mine, joined, state, early, codes, partner_far = lax.optimization_barrier(
        (near, mine, joined, state, early, codes, partner_far)
    )
    heads = range(queries.shape[1] // HD)
    asked = [choose(partner_far, [kv, *near], head) for head in heads]
    swapped = [swap_cores(block) for block in asked]
    theirs = [swap_cores(after(part, asked[-1])) for part in (joined, mine[2])]
    attn = None
    for head in heads:
        attn = attend_far(codes, queries, state, near, swapped[head], head, attn)
    return attn, mine, theirs, early


def projected(queries, keys, values, gates, o_proj, early):
    core = lax.axis_index("seq") % CORES

    def share_after(seen):
        return lax.dynamic_slice(after(o_proj, seen), (core * HD, 0), (HD, o_proj.shape[1]))

    pieces, mine, theirs, early = attend(
        queries, keys, values, gates, share_after, ring_x, early
    )
    rows = [pieces[0]] + [ring_x(piece, far) for piece, far in zip(pieces[1:], ORDER)]
    spot = jnp.stack([core, lax.axis_index("exp") % SIDE]).astype(jnp.int32)
    sums = project(spot, rows, o_proj, mine, theirs)
    total = sums[0].astype(jnp.float32)
    for piece, far in zip(sums[1:], ORDER):
        total = total + ring_y(piece, far).astype(jnp.float32)
    return total.astype(jnp.bfloat16), early


def expert_kernel(n_ff, rows_ref, gate_ref, up_ref, down_ref, out_ref, hidden_ref):
    step = pl.program_id(0)
    ff_tile = gate_ref.shape[2]

    @pl.when(step < n_ff)
    def _():
        rows = rows_ref[...]
        gate = jnp.dot(rows, gate_ref[0], preferred_element_type=jnp.float32)
        up = jnp.dot(rows, up_ref[0], preferred_element_type=jnp.float32)
        hidden = gate / (1.0 + jnp.exp(-gate)) * up
        cols = pl.ds(pl.multiple_of(step * ff_tile, ff_tile), ff_tile)
        hidden_ref[:, cols] = hidden.astype(jnp.bfloat16)

    @pl.when(step >= n_ff)
    def _():
        out_ref[...] = jnp.dot(
            hidden_ref[...], down_ref[0], preferred_element_type=jnp.float32
        ).astype(jnp.bfloat16)


def expert_rows(rows, w_gate, w_up, w_down):
    n_rows, width = rows.shape
    ff = w_gate.shape[2]
    ff_tile, out_tile = 256, 512
    n_ff, n_out = ff // ff_tile, width // out_tile

    def ff_at(i):
        return (0, 0, jnp.minimum(i, n_ff - 1))

    def out_at(i):
        return jnp.maximum(i - n_ff, 0)

    return pl.pallas_call(
        lambda *refs: expert_kernel(n_ff, *refs),
        grid=(n_ff + n_out,),
        in_specs=[
            pl.BlockSpec(memory_space=pltpu.VMEM),
            pl.BlockSpec((1, width, ff_tile), ff_at),
            pl.BlockSpec((1, width, ff_tile), ff_at),
            pl.BlockSpec((1, ff, out_tile), lambda i: (0, 0, out_at(i))),
        ],
        out_specs=pl.BlockSpec((n_rows, out_tile), lambda i: (0, out_at(i))),
        out_shape=pltpu.HBM((n_rows, width), jnp.bfloat16),
        scratch_shapes=[pltpu.VMEM((n_rows, ff), jnp.bfloat16)],
        compiler_params=pltpu.CompilerParams(vmem_limit_bytes=32 * 1024 * 1024),
        cost_estimate=pl.CostEstimate(
            flops=6 * n_rows * width * ff,
            bytes_accessed=2 * (2 * n_rows * width + 3 * width * ff),
            transcendentals=n_rows * ff,
        ),
        name="experts",
    )(rows, w_gate, w_up, w_down)


def slot_tables(routes, route_weights, n_experts, cap):
    n_tok, n_slots = routes.shape[0], n_experts * cap
    hit = jnp.zeros((n_tok, n_experts), jnp.bool_)
    weight = jnp.zeros((n_tok, n_experts), jnp.float32)
    expert_ids = lax.broadcasted_iota(jnp.int32, (n_tok, n_experts), 1)
    for k in range(routes.shape[1]):
        match = routes[:, k : k + 1] == expert_ids
        hit = jnp.logical_or(hit, match)
        weight = weight + jnp.where(match, route_weights[:, k : k + 1], 0.0)
    square = (n_tok, n_tok)
    ahead = lax.broadcasted_iota(jnp.int32, square, 0) > lax.broadcasted_iota(jnp.int32, square, 1)
    rank = jnp.dot(
        ahead.astype(jnp.bfloat16), hit.astype(jnp.bfloat16), preferred_element_type=jnp.float32
    )
    place = jnp.where(hit, rank, float(2 * n_tok)).astype(jnp.bfloat16)
    high = weight.astype(jnp.bfloat16)
    low = (weight - high.astype(jnp.float32)).astype(jnp.bfloat16)
    spread = lax.broadcasted_iota(jnp.int32, (n_experts, n_slots), 0) == (
        lax.broadcasted_iota(jnp.int32, (n_experts, n_slots), 1) // cap
    )
    wide = jnp.dot(
        jnp.concatenate([place, high, low], axis=0),
        spread.astype(jnp.bfloat16),
        preferred_element_type=jnp.float32,
    )
    slot_ids = lax.broadcasted_iota(jnp.int32, (n_tok, n_slots), 1) % cap
    taken = wide[:n_tok] == slot_ids.astype(jnp.float32)
    pick = taken.astype(jnp.bfloat16)
    mix = jnp.where(jnp.concatenate([taken, taken], axis=0), wide[n_tok:], 0.0)
    return pick.T, mix.astype(jnp.bfloat16)


def combine_kernel(mix_ref, rows_ref, out_ref):
    n_tok, tile = out_ref.shape
    cols = pl.ds(pl.multiple_of(pl.program_id(0) * tile, tile), tile)
    halves = jnp.dot(mix_ref[...], rows_ref[:, cols], preferred_element_type=jnp.float32)
    out_ref[...] = (halves[:n_tok] + halves[n_tok:]).astype(jnp.bfloat16)


def combine(mix, rows):
    n_rows, width = rows.shape
    n_tok, tile = mix.shape[0] // 2, 896
    return pl.pallas_call(
        combine_kernel,
        grid=(width // tile,),
        in_specs=[pl.BlockSpec(memory_space=pltpu.VMEM)] * 2,
        out_specs=pl.BlockSpec((n_tok, tile), lambda i: (0, i)),
        out_shape=jax.ShapeDtypeStruct((n_tok, width), jnp.bfloat16),
        compiler_params=pltpu.CompilerParams(vmem_limit_bytes=24 * 1024 * 1024),
        cost_estimate=pl.CostEstimate(
            flops=4 * n_tok * n_rows * width, bytes_accessed=2 * n_rows * width, transcendentals=0
        ),
        name="combine",
    )(mix, rows)


def per_device(
    queries,
    keys,
    values,
    gates,
    o_proj,
    residual,
    norm_gain,
    routes,
    route_weights,
    w_gate,
    w_up,
    w_down,
):
    tok_moe, width = residual.shape
    n_experts = w_gate.shape[0] * lax.axis_size("seq") * lax.axis_size("exp")
    cap = 2 * tok_moe * ROUTE_K // n_experts
    tables = slot_tables(routes, route_weights, n_experts, cap)
    summed, (place, mix) = projected(queries, keys, values, gates, o_proj, tables)
    residual_sum = residual.astype(jnp.float32) + summed.astype(jnp.float32)
    norm_scale = lax.rsqrt(jnp.mean(residual_sum * residual_sum, axis=-1, keepdims=True) + 1e-06)
    moe_in = (residual_sum * norm_scale * norm_gain).astype(jnp.bfloat16)
    senders = jnp.dot(place, moe_in, preferred_element_type=jnp.float32).astype(jnp.bfloat16)
    received = lax.all_to_all(
        senders.reshape(n_experts, cap, width),
        ("seq", "exp"),
        split_axis=0,
        concat_axis=0,
        tiled=True,
    )
    produced = expert_rows(received.reshape(n_experts * cap, width), w_gate, w_up, w_down)
    returned = lax.all_to_all(
        produced.reshape(n_experts, cap, width),
        ("seq", "exp"),
        split_axis=0,
        concat_axis=0,
        tiled=True,
    )
    moe_out = combine(mix, returned.reshape(n_experts * cap, width))
    return (summed, moe_out)


def solution(mesh):
    in_specs = (
        P("seq", "exp"),
        P("seq", "exp"),
        P("seq", "exp"),
        P(),
        P("exp", None),
        P(("seq", "exp"), None),
        P(),
        P(("seq", "exp"), None),
        P(("seq", "exp"), None),
        P(("seq", "exp"), None, None),
        P(("seq", "exp"), None, None),
        P(("seq", "exp"), None, None),
    )
    out_specs = (P(("seq", "exp"), None), P(("seq", "exp"), None))
    return jax.shard_map(
        per_device, mesh=mesh, in_specs=in_specs, out_specs=out_specs, check_vma=False
    )
```
